256 devices in a mesh: dp: 4 (over y_hi, core), ctx: 32 (over x, z), tp: 2 (over y_lo).
Axes of the slice: x: 4, y: 4 (y_hi: 2, y_lo: 2; y = y_hi * 2 + y_lo), z: 8, core: 2. Of those that a mesh axis runs over, the one named last changes fastest.
Arguments:
- queries: bfloat16 [128, 2, 64, 4096], P(('dp', 'ctx'), None, None, 'tp'), parts along dimension 0, may hold values from -8 to 8
- projected_key_rows: bfloat16 [128, 2, 64, 512], P(('dp', 'ctx'), None, None, 'tp'), parts along dimension 0, may hold values from -8 to 8
- values: bfloat16 [128, 2, 64, 512], P(('dp', 'ctx'), None, None, 'tp'), parts along dimension 0, may hold values from -6 to 6
- mixer_input: bfloat16 [128, 2, 64, 8192], P(('dp', 'ctx'), None, None, 'tp'), parts along dimension 0, may hold values from -6 to 6
- step_raw: bfloat16 [128, 2, 64, 8192], P(('dp', 'ctx'), None, None, 'tp'), parts along dimension 0, may hold values from -2 to 11
- gate_input: bfloat16 [128, 2, 64, 8192], P(('dp', 'ctx'), None, None, 'tp'), parts along dimension 0, may hold values from -6 to 6
- state_write: bfloat16 [128, 2, 64, 16], P(('dp', 'ctx')), parts along dimension 0, may hold values from -3 to 3
- state_read: bfloat16 [128, 2, 64, 16], P(('dp', 'ctx')), parts along dimension 0, may hold values from -3 to 3
- decay_log: float32 [16, 8192], P(None, 'tp'), may hold values from -2.3 to -1.2
- step_bias: float32 [8192], P('tp'), may hold values from -8 to 0
- conv_weight: float32 [4, 8192], P(None, 'tp'), may hold values from -3 to 3
- conv_bias: float32 [8192], P('tp'), may hold values from -0.5 to 0.5
- skip_gain: float32 [8192], P('tp'), may hold values from 0.5 to 1.5
Outputs:
- attended: bfloat16 [128, 2, 64, 4096], P(('dp', 'ctx'), None, None, 'tp'), parts along dimension 0
- selected: bfloat16 [128, 2, 64, 8192], P(('dp', 'ctx'), None, None, 'tp'), parts along dimension 0
The draws below stay inside these ranges and needn't reach their ends.
There are 4 independent parts, one for each index of `dp`. The reference program is written for one: setup_inputs(seed, part) draws one part's arguments, and reference() takes and returns one part's arrays. A program takes and returns all parts, laid end to end along the dimension named above; an argument that names none is the same for every part. Nothing has to cross between parts.
All inputs are finite; a program needn't handle non-finite values.
Results may differ from the reference program's by a relative error of at most 0.018.
Values may be sent and summed in bfloat16 or wider, within the bound.
No kernel may reach another device: no remote copies, remote signals or barrier semaphores. Data moves between devices by JAX's collectives and lax.ppermute only.
A program may use at most 128 MiB of HBM per device.

```python
import jax
import jax.numpy as jnp
from jax import lax

QUERY_HEADS = 32
KEY_VALUE_HEADS = 4
HEAD_SIZE = 128
SCAN_CHANNELS = 8192
NST = 16
KW = 4
BLOCK_TOKENS = 64
BLOCK_PAIRS = 32
WINDOW_TOKENS = 4096


def combined_rows(natural):
    blocks = natural.reshape((2 * BLOCK_PAIRS, BLOCK_TOKENS) + natural.shape[1:])
    return jnp.stack([blocks[:BLOCK_PAIRS], blocks[BLOCK_PAIRS:][::-1]], axis=1)


def aligned_rows(key):
    subkeys = jax.random.split(key, 9)
    spike_group = jax.random.randint(subkeys[5], (), 0, KEY_VALUE_HEADS)
    key_signs = jnp.where(jax.random.bernoulli(subkeys[6], 0.5, (HEAD_SIZE,)), 8.0, -8.0).astype(jnp.float32)
    loud_pos = jax.random.randint(subkeys[7], (8,), 0, WINDOW_TOKENS // 4)
    loud_rows = jnp.where(jax.random.bernoulli(subkeys[8], 0.5, (8, QUERY_HEADS // KEY_VALUE_HEADS, HEAD_SIZE)), 6.0, -6.0).astype(jnp.float32)
    return (spike_group, key_signs, loud_pos, loud_rows)


def draw_queries(key, part):
    spike_group, key_signs, loud_pos, loud_rows = aligned_rows(key)
    key = jax.random.fold_in(key, 11)
    repeat_factor = QUERY_HEADS // KEY_VALUE_HEADS
    head_list = spike_group * repeat_factor + jnp.arange(repeat_factor, dtype=jnp.int32)
    entry_list = jnp.clip(jax.random.normal(key, (WINDOW_TOKENS, QUERY_HEADS, HEAD_SIZE), jnp.float32), -4.0, 4.0)
    entry_list = entry_list.at[loud_pos[:, None], head_list[None, :]].set(loud_rows)
    return combined_rows(entry_list.reshape(WINDOW_TOKENS, QUERY_HEADS * HEAD_SIZE)).astype(jnp.bfloat16)


def draw_projected_key_rows(key, part):
    spike_group, key_signs, loud_pos, loud_rows = aligned_rows(key)
    key = jax.random.fold_in(key, 13)
    entry_list = jnp.clip(jax.random.normal(key, (WINDOW_TOKENS, KEY_VALUE_HEADS, HEAD_SIZE), jnp.float32), -4.0, 4.0)
    entry_list = entry_list.at[WINDOW_TOKENS - 1, spike_group].set(key_signs)
    return combined_rows(entry_list.reshape(WINDOW_TOKENS, KEY_VALUE_HEADS * HEAD_SIZE)).astype(jnp.bfloat16)


def draw_step_raw(key, part):
    key = jax.random.fold_in(key, 21)
    subkeys = jax.random.split(key, 5)
    random_noise = jnp.clip(0.4 * jax.random.normal(subkeys[0], (WINDOW_TOKENS, SCAN_CHANNELS), jnp.float32), -0.8, 0.8)
    segment_len = BLOCK_TOKENS // 2
    offsets = jax.random.uniform(subkeys[1], (WINDOW_TOKENS // segment_len, SCAN_CHANNELS), jnp.float32, -1.0, 1.0)
    shifted_rows = jnp.repeat(offsets, segment_len, axis=0)
    flagged_rows = jax.random.randint(subkeys[2], (6,), 0, WINDOW_TOKENS)
    chosen = jax.random.bernoulli(subkeys[3], 0.4, (6, SCAN_CHANNELS)).astype(jnp.float32)
    raised_values = jax.random.uniform(subkeys[4], (6, SCAN_CHANNELS), jnp.float32, 7.0, 9.0) * chosen
    spike_rows = jnp.zeros((WINDOW_TOKENS, SCAN_CHANNELS), jnp.float32).at[flagged_rows].set(raised_values)
    return combined_rows(random_noise + shifted_rows + spike_rows).astype(jnp.bfloat16)


def draw_step_bias(key, part):
    key = jax.random.fold_in(key, 31)
    subkeys = jax.random.split(key, 3)
    share = 0.5
    slow_mask = jax.random.bernoulli(subkeys[0], share, (SCAN_CHANNELS,))
    slow_values = jax.random.uniform(subkeys[1], (SCAN_CHANNELS,), jnp.float32, -8.0, -6.5)
    spread_values = jax.random.uniform(subkeys[2], (SCAN_CHANNELS,), jnp.float32, -6.5, 0.0)
    return jnp.where(slow_mask, slow_values, spread_values).astype(jnp.float32)


def block_scale(key, extent, shards, smallest, top_value):
    factor_of, own = 1.0, jax.random.fold_in(key, 6)
    for axis_at, parts in shards:
        draws = jnp.exp(jax.random.uniform(jax.random.fold_in(own, axis_at), (parts,), jnp.float32, smallest / len(shards), top_value / len(shards)))
        factor_of = factor_of * jnp.repeat(draws, extent[axis_at] // parts).reshape([-1 if axis == axis_at else 1 for axis in range(len(extent))])
    return factor_of


def scatter_about(key, extent, deviation, limit, cuts=(), held_as=jnp.bfloat16):
    result = jax.random.normal(key, extent, jnp.float32) * deviation
    if len(cuts) > 0:
        result = block_scale(key, extent, cuts, -0.22, 0.18) * result
    return jnp.clip(result, min=-limit, max=limit).astype(held_as)


def setup_inputs(seed: int = 0, part: int = 0) -> dict:
    keys = jax.random.split(jax.random.key(seed), 14)
    part_keys = jax.random.split(jax.random.fold_in(keys[13], part), 14)
    return {
        "queries": draw_queries(jax.random.fold_in(jax.random.fold_in(keys[13], part), 71), part),
        "projected_key_rows": draw_projected_key_rows(jax.random.fold_in(jax.random.fold_in(keys[13], part), 71), part),
        "values": scatter_about(part_keys[2], (BLOCK_PAIRS, 2, BLOCK_TOKENS, KEY_VALUE_HEADS * HEAD_SIZE), 1.0, 6.0, ((0, 32), (3, 2))),
        "mixer_input": scatter_about(part_keys[3], (BLOCK_PAIRS, 2, BLOCK_TOKENS, SCAN_CHANNELS), 1.0, 6.0, ((0, 32), (3, 2))),
        "step_raw": draw_step_raw(jax.random.fold_in(jax.random.fold_in(keys[13], part), 71), part),
        "gate_input": scatter_about(part_keys[5], (BLOCK_PAIRS, 2, BLOCK_TOKENS, SCAN_CHANNELS), 1.0, 6.0, ((0, 32), (3, 2))),
        "state_write": scatter_about(part_keys[6], (BLOCK_PAIRS, 2, BLOCK_TOKENS, NST), 0.5, 3.0, ((0, 32),)),
        "state_read": scatter_about(part_keys[7], (BLOCK_PAIRS, 2, BLOCK_TOKENS, NST), 0.5, 3.0, ((0, 32),)),
        "decay_log": jnp.clip(-2.3 + 1.0999999 * jax.random.uniform(keys[8], (NST, SCAN_CHANNELS), jnp.float32) ** block_scale(keys[8], (NST, SCAN_CHANNELS), ((1, 2),), -0.2, 0.2), -2.3, -1.2),
        "step_bias": draw_step_bias(jax.random.fold_in(keys[13], 71), part),
        "conv_weight": scatter_about(keys[10], (KW, SCAN_CHANNELS), KW ** -0.5, 3.0, ((1, 2),), jnp.float32),
        "conv_bias": jnp.clip(jax.random.uniform(keys[11], (SCAN_CHANNELS,), jnp.float32, -0.5, 0.5) * block_scale(keys[11], (SCAN_CHANNELS,), ((0, 2),), -0.4, 0.0), -0.5, 0.5),
        "skip_gain": jnp.clip(0.5 + 1.0 * jax.random.uniform(keys[12], (SCAN_CHANNELS,), jnp.float32) ** block_scale(keys[12], (SCAN_CHANNELS,), ((0, 2),), -0.2, 0.2), 0.5, 1.5),
    }


def unfold_rows(folded):
    first_half = folded[:, 0]
    second_half = folded[::-1, 1]
    joined = jnp.concatenate([first_half, second_half], axis=0)
    return joined.reshape((joined.shape[0] * joined.shape[1],) + joined.shape[2:])


def fold(natural):
    blocks = natural.reshape((2 * BLOCK_PAIRS, BLOCK_TOKENS) + natural.shape[1:])
    return jnp.stack([blocks[:BLOCK_PAIRS], blocks[BLOCK_PAIRS:][::-1]], axis=1)


def attention(queries, projected_key_rows, values):
    repeat_factor = QUERY_HEADS // KEY_VALUE_HEADS
    scale = HEAD_SIZE ** -0.5
    key_widened = unfold_rows(projected_key_rows).reshape(WINDOW_TOKENS, KEY_VALUE_HEADS, HEAD_SIZE).astype(jnp.float32)
    value_widened = unfold_rows(values).reshape(WINDOW_TOKENS, KEY_VALUE_HEADS, HEAD_SIZE).astype(jnp.float32)
    query_block_list = unfold_rows(queries).reshape(WINDOW_TOKENS // BLOCK_TOKENS, BLOCK_TOKENS, KEY_VALUE_HEADS, repeat_factor, HEAD_SIZE)
    key_pos = jnp.arange(WINDOW_TOKENS, dtype=jnp.int32)

    def one_block(block_index):
        query_block = lax.dynamic_index_in_dim(query_block_list, block_index, 0, keepdims=False).astype(jnp.float32)
        query_pos = block_index * BLOCK_TOKENS + jnp.arange(BLOCK_TOKENS, dtype=jnp.int32)
        scores = jnp.einsum("qgrd,kgd->qgrk", query_block, key_widened) * scale
        causal_permitted = key_pos[None, None, None, :] <= query_pos[:, None, None, None]
        scores = jnp.where(causal_permitted, scores, -jnp.inf)
        row_max = jnp.max(scores, axis=-1, keepdims=True)
        weights = jnp.exp(scores - row_max)
        totals = jnp.sum(weights, axis=-1)
        rounded = lax.optimization_barrier(weights.astype(jnp.bfloat16)).astype(jnp.float32)
        mixed = jnp.einsum("qgrk,kgd->qgrd", rounded, value_widened)
        return (mixed / totals[..., None]).astype(jnp.bfloat16)

    produced = lax.map(one_block, jnp.arange(WINDOW_TOKENS // BLOCK_TOKENS, dtype=jnp.int32))
    return fold(produced.reshape(WINDOW_TOKENS, QUERY_HEADS * HEAD_SIZE))


def selective(mixer_input, step_raw, gate_input, state_write, state_read, decay_log, step_bias, conv_weight, conv_bias, skip_gain):
    raw_input = unfold_rows(mixer_input).astype(jnp.float32)
    conv_width = conv_weight.shape[0]
    padded = jnp.concatenate([jnp.zeros((conv_width - 1, SCAN_CHANNELS), jnp.float32), raw_input], axis=0)
    conv_sum = conv_bias + sum(conv_weight[lag_index] * padded[lag_index:lag_index + WINDOW_TOKENS] for lag_index in range(conv_width))
    signal = jax.nn.silu(conv_sum)
    step_rate = jax.nn.softplus(unfold_rows(step_raw).astype(jnp.float32) + step_bias)
    decay_rate = -jnp.exp(decay_log)
    writes = unfold_rows(state_write).astype(jnp.float32)
    reads = unfold_rows(state_read).astype(jnp.float32)

    def advance(hidden, step_row):
        signal_row, rate_row, write_row, read_row = step_row
        hidden = jnp.exp(rate_row[None, :] * decay_rate) * hidden + (rate_row * signal_row)[None, :] * write_row[:, None]
        return hidden, jnp.sum(read_row[:, None] * hidden, axis=0)

    final_state, outputs = lax.scan(advance, jnp.zeros((NST, SCAN_CHANNELS), jnp.float32), (signal, step_rate, writes, reads))
    mixed = (outputs + skip_gain * signal) * jax.nn.silu(unfold_rows(gate_input).astype(jnp.float32))
    return fold(mixed.astype(jnp.bfloat16))


def reference(queries, projected_key_rows, values, mixer_input, step_raw, gate_input, state_write, state_read, decay_log, step_bias, conv_weight, conv_bias, skip_gain):
    attended = attention(queries, projected_key_rows, values)
    selected = selective(mixer_input, step_raw, gate_input, state_write, state_read, decay_log, step_bias, conv_weight, conv_bias, skip_gain)
    return (attended, selected)
```

```python
import functools

import jax
import jax.numpy as jnp
from jax import lax
from jax.experimental import pallas as pl
from jax.experimental.pallas import tpu as pltpu
from jax.sharding import PartitionSpec as P

HEAD = 128
NST = 16
LOG2E = 1.4426950408889634
TILE = 512
LANES = 128
MSG_ROWS = 40
ROW = 8
BIG_NEG = -1e30
F32 = jnp.float32
BF16 = jnp.bfloat16


def dot_nt(a, b):
    return lax.dot_general(a, b, (((1,), (1,)), ((), ())), preferred_element_type=F32)


def dot_nn(a, b):
    return lax.dot_general(a, b, (((1,), (0,)), ((), ())), preferred_element_type=F32)


def attend_kernel(rank_ref, q_ref, kv_ref, o_ref, qs, acc, top, *, block, pairs, heads):
    rank = rank_ref[0]
    rows = heads * block
    part = 128
    scale = LOG2E * HEAD ** -0.5
    for b in range(2):
        for h in range(heads):
            scaled = q_ref[b, :, h * HEAD:(h + 1) * HEAD].astype(F32) * scale
            high = scaled.astype(BF16)
            low = (scaled - high.astype(F32)).astype(BF16)
            qs[pl.ds(b * rows + h * block, block), :HEAD] = high
            qs[pl.ds(b * rows + h * block, block), HEAD:] = low

    def visit(b, keys, vals, mask_of, first):
        both_keys = jnp.concatenate([keys, keys], axis=1)
        with_ones = jnp.concatenate([vals, jnp.ones_like(vals)], axis=1)

        def step(k, carry):
            at = pl.multiple_of(b * rows + k * part, part)
            scores = dot_nt(qs[pl.ds(at, part)], both_keys)
            if mask_of is not None:
                scores = mask_of(scores)
            best = jnp.max(scores, axis=1, keepdims=True)
            if not first:
                old = top[pl.ds(at, part), :1]
                best = jnp.maximum(best, old)
            weights = jnp.exp2(scores - best).astype(BF16)
            added = dot_nn(weights, with_ones)
            if not first:
                added = added + acc[pl.ds(at, part)] * jnp.exp2(old - best)
            acc[pl.ds(at, part)] = added
            top[pl.ds(at, part)] = jnp.broadcast_to(best, (part, LANES))
            return carry

        lax.fori_loop(0, rows // part, step, 0)

    def load(row, what, half):
        return kv_ref[pl.ds(row * ROW, ROW), what, half].reshape(ROW * block, HEAD)

    mine = rank // ROW
    place = rank % ROW
    span = ROW * block

    def position(shape):
        token = lax.broadcasted_iota(jnp.int32, shape, 0) % block
        key = lax.broadcasted_iota(jnp.int32, shape, 1)
        return token, key

    def early_mask(scores):
        token, key = position(scores.shape)
        return jnp.where(key <= token + place * block, scores, BIG_NEG)

    def late_mask(scores):
        token, key = position(scores.shape)
        key = key - span
        own = (key >= place * block) & (key <= token + place * block)
        return jnp.where((key < 0) | (key >= (place + 1) * block) | own, scores, BIG_NEG)

    def all_keys(row, what):
        return jnp.concatenate([load(row, what, 0), load(row, what, 1)], axis=0)

    visit(0, load(mine, 0, 0), load(mine, 1, 0), early_mask, True)
    visit(1, all_keys(mine, 0), all_keys(mine, 1), late_mask, True)

    def other(row, carry):
        @pl.when(row > mine)
        def _():
            visit(1, all_keys(row, 0), all_keys(row, 1), None, False)

        @pl.when(row < mine)
        def _():
            keys, vals = load(row, 0, 0), load(row, 1, 0)
            visit(0, keys, vals, None, False)
            visit(1, keys, vals, None, False)

        return carry

    lax.fori_loop(0, pairs // ROW, other, 0)
    for b in range(2):
        for h in range(heads):
            done = acc[pl.ds(b * rows + h * block, block)]
            o_ref[b, :, h * HEAD:(h + 1) * HEAD] = (done[:, :HEAD] / done[:, HEAD:]).astype(BF16)


def attend(rank, queries, kv):
    _, block, width = queries.shape
    pairs = kv.shape[0]
    groups = kv.shape[-1] // HEAD
    heads = width // HEAD // groups
    return pl.pallas_call(
        functools.partial(attend_kernel, block=block, pairs=pairs, heads=heads),
        grid_spec=pltpu.PrefetchScalarGridSpec(
            num_scalar_prefetch=1,
            grid=(groups,),
            in_specs=[
                pl.BlockSpec((2, block, heads * HEAD), lambda g, r: (0, 0, g)),
                pl.BlockSpec((pairs, 2, 2, block, HEAD), lambda g, r: (0, 0, 0, 0, g)),
            ],
            out_specs=pl.BlockSpec((2, block, heads * HEAD), lambda g, r: (0, 0, g)),
            scratch_shapes=[
                pltpu.VMEM((2 * heads * block, 2 * HEAD), BF16),
                pltpu.VMEM((2 * heads * block, 2 * HEAD), F32),
                pltpu.VMEM((2 * heads * block, LANES), F32),
            ],
        ),
        out_shape=jax.ShapeDtypeStruct(queries.shape, BF16),
        compiler_params=pltpu.CompilerParams(vmem_limit_bytes=40 * 2**20),
        cost_estimate=pl.CostEstimate(flops=2 * 10**9, bytes_accessed=6 * 10**6, transcendentals=5 * 10**6),
        name="attend",
    )(rank, queries, kv)


def softplus(v):
    small = jnp.exp(-jnp.abs(v))
    return jnp.maximum(v, 0.0) + jnp.log1p(small)


def silu(v):
    return v / (1.0 + jnp.exp(-v))


def summary_kernel(
    mix_ref, halo_ref, step_ref, bias_ref, taps_ref, conv_bias_ref, decay_ref, writes_ref,
    rate_ref, signal_ref, msg_ref, ext, spread, *, block, taps
):
    decay = -jnp.exp(decay_ref[...]) * LOG2E
    row = lax.broadcasted_iota(jnp.int32, (block, 2 * block), 0)
    col = lax.broadcasted_iota(jnp.int32, (block, 2 * block), 1) % block
    later = (col > row).astype(BF16)
    states, ends = [], []
    for b in range(2):
        ext[b, :8] = halo_ref[b]
        ext[b, 8:] = mix_ref[b].astype(F32)
        summed = conv_bias_ref[...]
        for m in range(taps):
            summed = summed + taps_ref[m:m + 1] * ext[b, pl.ds(8 - taps + 1 + m, block)]
        signal = silu(summed)
        rate = softplus(step_ref[b].astype(F32) + bias_ref[...])
        rate_ref[b] = rate
        signal_ref[b] = signal
        inflow = (rate * signal).astype(BF16)
        high = rate.astype(BF16)
        low = (rate - high.astype(F32)).astype(BF16)
        remaining = dot_nn(later, jnp.concatenate([high, low], axis=0))
        ends.append(remaining[:1] + rate[:1])
        for n in range(NST):
            kept = jnp.exp2(decay[n:n + 1] * remaining).astype(BF16)
            spread[n * block:(n + 1) * block] = kept * inflow
        states.append(dot_nn(writes_ref[b], spread[...]))
    rows = []
    for end in ends:
        high = end.astype(BF16).astype(F32)
        rows += [high, end - high]
    rows.append(jnp.zeros((8 - len(rows), rows[0].shape[1]), F32))
    message = jnp.concatenate(states + rows, axis=0).astype(BF16)
    for j in range(message.shape[1] // LANES):
        msg_ref[j] = message[:, j * LANES:(j + 1) * LANES]


def summarize(mix, halo, step, bias, taps, conv_bias, decay_log, writes):
    _, block, channels = mix.shape
    tile = min(TILE, channels)
    seq = pl.BlockSpec((2, block, tile), lambda c: (0, 0, c))
    line = lambda rows: pl.BlockSpec((rows, tile), lambda c: (0, c))
    return pl.pallas_call(
        functools.partial(summary_kernel, block=block, taps=taps.shape[0]),
        grid=(channels // tile,),
        in_specs=[
            seq,
            pl.BlockSpec((2, 8, tile), lambda c: (0, 0, c)),
            seq,
            line(1),
            line(taps.shape[0]),
            line(1),
            line(NST),
            pl.BlockSpec((2, NST, NST * block), lambda c: (0, 0, 0)),
        ],
        out_specs=[seq, seq, pl.BlockSpec((tile // LANES, MSG_ROWS, LANES), lambda c: (c, 0, 0))],
        out_shape=[
            jax.ShapeDtypeStruct(mix.shape, F32),
            jax.ShapeDtypeStruct(mix.shape, F32),
            jax.ShapeDtypeStruct((channels // LANES, MSG_ROWS, LANES), BF16),
        ],
        scratch_shapes=[
            pltpu.VMEM((2, 8 + block, tile), F32),
            pltpu.VMEM((NST * block, tile), BF16),
        ],
        compiler_params=pltpu.CompilerParams(vmem_limit_bytes=32 * 2**20),
        cost_estimate=pl.CostEstimate(flops=10**8, bytes_accessed=7 * 10**6, transcendentals=9 * 10**6),
        name="summarize",
    )(mix, halo, step, bias, taps, conv_bias, decay_log, writes)


def prefix_kernel(msg_ref, decay_ref, out_ref, *, pairs):
    decay = -jnp.exp(decay_ref[...]) * LOG2E

    def hop(j, state, half):
        out_ref[j, half * NST:(half + 1) * NST] = state.astype(BF16)
        piece = msg_ref[j].astype(F32)
        end = piece[2 * NST + 2 * half:2 * NST + 2 * half + 1] + piece[2 * NST + 2 * half + 1:2 * NST + 2 * half + 2]
        return jnp.exp2(decay * end) * state + piece[half * NST:(half + 1) * NST]

    state = jnp.zeros(decay.shape, F32)
    state = lax.fori_loop(0, pairs, lambda j, s: hop(j, s, 0), state, unroll=8)
    lax.fori_loop(0, pairs, lambda j, s: hop(pairs - 1 - j, s, 1), state, unroll=8)


def prefix(msg, decay_part):
    pairs = msg.shape[0]
    return pl.pallas_call(
        functools.partial(prefix_kernel, pairs=pairs),
        out_shape=jax.ShapeDtypeStruct((pairs, 2 * NST, LANES), BF16),
        cost_estimate=pl.CostEstimate(flops=10**6, bytes_accessed=6 * 10**5, transcendentals=10**5),
        name="prefix",
    )(msg, decay_part)


def scan_kernel(
    rate_ref, signal_ref, gate_ref, start_ref, decay_ref, skip_ref, writes_ref, reads_ref,
    out_ref, inflow, held, *, block
):
    tile = rate_ref.shape[2]
    cols = tile // LANES
    group = 16
    decay = -jnp.exp(decay_ref[...]) * LOG2E
    for b in range(2):
        inflow[b] = rate_ref[b] * signal_ref[b]

    def start(b):
        return jnp.concatenate(
            [start_ref[j, b * NST:(b + 1) * NST].astype(F32) for j in range(cols)], axis=1
        )

    def some(g, states):
        states = list(states)
        for k in range(group):
            t = g * group + k
            for b in range(2):
                kept = jnp.exp2(decay * rate_ref[b, pl.ds(t, 1)])
                write = jnp.concatenate([writes_ref[b, t]] * cols, axis=1)
                states[b] = kept * states[b] + inflow[b, pl.ds(t, 1)] * write
                held[b, k * NST:(k + 1) * NST] = states[b].astype(BF16)
        at = pl.multiple_of(g * group, group)
        for b in range(2):
            summed = dot_nn(reads_ref[b, g], held[b])
            mixed = summed + skip_ref[...] * signal_ref[b, pl.ds(at, group)]
            gate = gate_ref[b, pl.ds(at, group)].astype(F32)
            out_ref[b, pl.ds(at, group)] = (mixed * silu(gate)).astype(BF16)
        return tuple(states)

    lax.fori_loop(0, block // group, some, (start(0), start(1)))


def scan(rate, signal, gate, start, decay_log, skip, writes, reads):
    _, block, channels = rate.shape
    tile = min(TILE, channels)
    seq = pl.BlockSpec((2, block, tile), lambda c: (0, 0, c))
    line = lambda rows: pl.BlockSpec((rows, tile), lambda c: (0, c))
    return pl.pallas_call(
        functools.partial(scan_kernel, block=block),
        grid=(channels // tile,),
        in_specs=[
            seq,
            seq,
            seq,
            pl.BlockSpec((tile // LANES, 2 * NST, LANES), lambda c: (c, 0, 0)),
            line(NST),
            line(1),
            pl.BlockSpec(writes.shape, lambda c: (0, 0, 0, 0)),
            pl.BlockSpec(reads.shape, lambda c: (0, 0, 0, 0)),
        ],
        out_specs=seq,
        out_shape=jax.ShapeDtypeStruct(gate.shape, BF16),
        scratch_shapes=[
            pltpu.VMEM((2, block, tile), F32),
            pltpu.VMEM((2, 16 * NST, tile), BF16),
        ],
        compiler_params=pltpu.CompilerParams(vmem_limit_bytes=32 * 2**20),
        cost_estimate=pl.CostEstimate(flops=10**8, bytes_accessed=8 * 10**6, transcendentals=9 * 10**6),
        name="scan",
    )(rate, signal, gate, start, decay_log, skip, writes, reads)


def body(
    queries,
    projected_key_rows,
    values,
    mixer_input,
    step_raw,
    gate_input,
    state_write,
    state_read,
    decay_log,
    step_bias,
    conv_weight,
    conv_bias,
    skip_gain,
):
    rank = lax.axis_index("ctx")
    count = lax.axis_size("ctx")
    block = queries.shape[2]
    taps = conv_weight.shape[0]
    eye = jnp.eye(NST, dtype=BF16)

    halves = mixer_input[0]
    tails = halves[:, block - (taps - 1):]
    forward = [(i, i + 1) for i in range(count - 1)]
    backward = [(i + 1, i) for i in range(count - 1)]
    before_first = lax.ppermute(tails[0], "ctx", forward)
    before_second = lax.ppermute(tails[1], "ctx", backward)
    before_second = jnp.where(rank == count - 1, tails[0], before_second)
    halo = jnp.pad(
        jnp.stack([before_first, before_second]).astype(F32), ((0, 0), (8 - taps + 1, 0), (0, 0))
    )

    kv = jnp.stack([projected_key_rows[0], values[0]])
    kv_all = lax.all_gather(kv, "ctx")

    writes = state_write[0]
    write_mat = (eye[None, :, :, None] * jnp.swapaxes(writes, 1, 2)[:, None]).reshape(
        2, NST, NST * block
    )
    write_wide = jnp.broadcast_to(writes.astype(F32)[..., None], (2, block, NST, LANES))
    read_mat = (
        jnp.eye(16, dtype=BF16)[None, None, :, :, None]
        * state_read[0].reshape(2, block // 16, 1, 16, NST)
    ).reshape(2, block // 16, 16, 16 * NST)

    rate, signal, msg = summarize(
        halves, halo, step_raw[0], step_bias[None], conv_weight, conv_bias[None], decay_log, write_mat
    )
    msg = lax.all_to_all(msg, "ctx", 0, 0, tiled=True)
    decay_part = lax.dynamic_slice_in_dim(decay_log, rank * LANES, LANES, 1)
    start = lax.all_to_all(prefix(msg, decay_part), "ctx", 0, 0, tiled=True)
    selected = scan(
        rate, signal, gate_input[0], start, decay_log, skip_gain[None], write_wide, read_mat
    )
    attended = attend(jnp.reshape(rank, (1,)).astype(jnp.int32), queries[0], kv_all)
    return (attended[None], selected[None])


def solution(mesh):
    rows = P(("dp", "ctx"), None, None, "tp")
    shared = P(("dp", "ctx"), None, None, None)
    return jax.shard_map(
        body,
        mesh=mesh,
        in_specs=(rows,) * 6 + (shared,) * 2
        + (P(None, "tp"), P("tp"), P(None, "tp"), P("tp"), P("tp")),
        out_specs=(rows, rows),
        check_vma=False,
    )
```

```python
import functools

import jax
import jax.numpy as jnp
from jax import lax
from jax.experimental import pallas as pl
from jax.experimental.pallas import tpu as pltpu
from jax.sharding import PartitionSpec as P

HEAD = 128
NST = 16
LOG2E = 1.4426950408889634
TILE = 512
WIDE = 1024
LANES = 128
MSG_ROWS = 40
ROW = 8
BIG_NEG = -1e30
VMEM = 56 * 2**20
F32 = jnp.float32
BF16 = jnp.bfloat16


def dot_nt(a, b):
    return lax.dot_general(a, b, (((1,), (1,)), ((), ())), preferred_element_type=F32)


def dot_nn(a, b):
    return lax.dot_general(a, b, (((1,), (0,)), ((), ())), preferred_element_type=F32)


def attend_kernel(where_ref, q_ref, own_ref, other_ref, o_ref, qs, acc, top, kvs, sems, *, block, heads, turns):
    mine, place, odd, core = where_ref[0], where_ref[1], where_ref[2], where_ref[3]
    rows = heads * block
    span = ROW * block
    scale = LOG2E * HEAD ** -0.5

    def fetch(row, source=own_ref):
        return pltpu.make_async_copy(source.at[:, (row + odd) % 2], kvs.at[row], sems.at[row])

    for d in range(turns):
        row = (mine + d) % turns

        @pl.when(row // 2 == core)
        def _():
            fetch(row, own_ref).start()

        @pl.when(row // 2 != core)
        def _():
            fetch(row, other_ref).start()

    for b in range(2):
        for h in range(heads):
            scaled = q_ref[b, :, h * HEAD:(h + 1) * HEAD].astype(F32) * scale
            high = scaled.astype(BF16)
            low = (scaled - high.astype(F32)).astype(BF16)
            qs[pl.ds(b * rows + h * block, block), :HEAD] = high
            qs[pl.ds(b * rows + h * block, block), HEAD:] = low

    def score(b, row, half):
        keys = kvs[row, :, 0, half].reshape(span, HEAD)
        at = pl.multiple_of(b * rows, rows)
        return dot_nt(qs[pl.ds(at, rows)], jnp.concatenate([keys, keys], axis=1))

    def update(b, row, half, scores, first):
        vals = kvs[row, :, 1, half].reshape(span, HEAD)
        at = pl.multiple_of(b * rows, rows)
        best = jnp.broadcast_to(jnp.max(scores, axis=1, keepdims=True), (rows, LANES))
        if not first:
            old = top[pl.ds(at, rows)]
            best = jnp.maximum(best, old)
        weights = jnp.exp2(scores - jnp.concatenate([best] * (span // LANES), axis=1)).astype(BF16)
        added = dot_nn(weights, jnp.concatenate([vals, jnp.ones_like(vals)], axis=1))
        if not first:
            factor = jnp.exp2(old - best)
            added = added + acc[pl.ds(at, rows)] * jnp.concatenate([factor, factor], axis=1)
        acc[pl.ds(at, rows)] = added
        top[pl.ds(at, rows)] = best

    token = lax.broadcasted_iota(jnp.int32, (rows, span), 0) % block
    key = lax.broadcasted_iota(jnp.int32, (rows, span), 1)
    upto = key <= token + place * block
    after = (key >= (place + 1) * block) | ((key >= place * block) & upto)

    fetch(mine).wait()
    early = score(0, mine, 0)
    late = score(1, mine, 0)
    own = score(1, mine, 1)
    update(0, mine, 0, jnp.where(upto, early, BIG_NEG), True)
    update(1, mine, 0, late, True)
    update(1, mine, 1, jnp.where(after, own, BIG_NEG), False)

    def other(d, carry):
        row = (mine + d) % turns
        later = (row > mine).astype(jnp.int32)
        fetch(row).wait()
        late = score(1, row, 0)
        second = score(later, row, later)
        update(1, row, 0, late, False)
        update(later, row, later, second, False)
        return carry

    lax.fori_loop(1, turns, other, 0)
    for b in range(2):
        for h in range(heads):
            done = acc[pl.ds(b * rows + h * block, block)]
            o_ref[b, :, h * HEAD:(h + 1) * HEAD] = (done[:, :HEAD] / done[:, HEAD:]).astype(BF16)


def attend(where, queries, own, other):
    _, block, width = queries.shape
    heads = width // HEAD
    turns = 2 * own.shape[1]
    return pl.pallas_call(
        functools.partial(attend_kernel, block=block, heads=heads, turns=turns),
        in_specs=[
            pl.BlockSpec(memory_space=pltpu.SMEM),
            pl.BlockSpec(memory_space=pltpu.VMEM),
            pl.BlockSpec(memory_space=pl.ANY),
            pl.BlockSpec(memory_space=pl.ANY),
        ],
        out_specs=pl.BlockSpec(memory_space=pltpu.VMEM),
        scratch_shapes=[
            pltpu.VMEM((2 * heads * block, 2 * HEAD), BF16),
            pltpu.VMEM((2 * heads * block, 2 * HEAD), F32),
            pltpu.VMEM((2 * heads * block, LANES), F32),
            pltpu.VMEM((turns, ROW, 2, 2, block, HEAD), BF16),
            pltpu.SemaphoreType.DMA((turns,)),
        ],
        out_shape=jax.ShapeDtypeStruct(queries.shape, BF16),
        compiler_params=pltpu.CompilerParams(vmem_limit_bytes=VMEM),
        cost_estimate=pl.CostEstimate(flops=10**9, bytes_accessed=3 * 10**6, transcendentals=3 * 10**6),
        name="attend",
    )(where, queries, own, other)


def split_kernel(odd_ref, keys_ref, values_ref, first_ref, second_ref):
    odd = odd_ref[0]
    for k, out in enumerate((first_ref, second_ref)):
        at = pl.multiple_of(((odd + k) % 2) * HEAD, HEAD)
        out[0] = keys_ref[:, :, pl.ds(at, HEAD)]
        out[1] = values_ref[:, :, pl.ds(at, HEAD)]


def split(odd, keys, values):
    half, block, _ = keys.shape
    part = jax.ShapeDtypeStruct((2, half, block, HEAD), BF16)
    return pl.pallas_call(
        split_kernel,
        in_specs=[pl.BlockSpec(memory_space=pltpu.SMEM)] + [pl.BlockSpec(memory_space=pltpu.VMEM)] * 2,
        out_specs=[pl.BlockSpec(memory_space=pltpu.VMEM)] * 2,
        out_shape=[part, part],
        name="split",
    )(odd, keys, values)


def after_kernel(*refs):
    del refs


def after(arrays, other):
    anywhere = pl.BlockSpec(memory_space=pl.ANY)
    return pl.pallas_call(
        after_kernel,
        in_specs=[anywhere] * (len(arrays) + 1),
        out_specs=[anywhere] * len(arrays),
        out_shape=[jax.ShapeDtypeStruct(a.shape, a.dtype) for a in arrays],
        input_output_aliases={i: i for i in range(len(arrays))},
        name="after",
    )(*arrays, other)


def assemble_kernel(place_ref, *refs):
    pieces, out_ref, sems = refs[:ROW], refs[-2], refs[-1]

    def copy(k):
        at = (place_ref[0] + k) % ROW
        return pltpu.make_async_copy(pieces[k], out_ref.at[at], sems.at[k])

    for k in range(ROW):
        copy(k).start()
    for k in range(ROW):
        copy(k).wait()


def assemble(place, pieces, other):
    anywhere = pl.BlockSpec(memory_space=pl.ANY)
    return pl.pallas_call(
        assemble_kernel,
        in_specs=[pl.BlockSpec(memory_space=pltpu.SMEM)] + [anywhere] * (ROW + 1),
        out_specs=pl.BlockSpec(memory_space=pltpu.VMEM),
        out_shape=jax.ShapeDtypeStruct((ROW,) + pieces[0].shape, BF16),
        scratch_shapes=[pltpu.SemaphoreType.DMA((ROW,))],
        name="assemble",
    )(place, *pieces, other)


def pack_kernel(last_ref, first_ref, second_ref, before_ref, after_ref, tail_ref, pair_ref, halo_ref):
    pair_ref[0] = first_ref[...]
    pair_ref[1] = second_ref[...]
    taps = before_ref.shape[0]
    blank = jnp.zeros((8 - taps, before_ref.shape[1]), F32)
    halo_ref[0] = jnp.concatenate([blank, before_ref[...].astype(F32)], axis=0)
    follow = jnp.where(last_ref[0] == 1, tail_ref[...].astype(F32), after_ref[...].astype(F32))
    halo_ref[1] = jnp.concatenate([blank, follow], axis=0)


def pack(last, first, second, before, after, tail):
    vmem = pl.BlockSpec(memory_space=pltpu.VMEM)
    return pl.pallas_call(
        pack_kernel,
        in_specs=[pl.BlockSpec(memory_space=pltpu.SMEM)] + [vmem] * 5,
        out_specs=[vmem, vmem],
        out_shape=[
            jax.ShapeDtypeStruct((2,) + first.shape, BF16),
            jax.ShapeDtypeStruct((2, 8, before.shape[1]), F32),
        ],
        name="pack",
    )(last, first, second, before, after, tail)


def softplus(v):
    small = jnp.exp(-jnp.abs(v))
    return jnp.maximum(v, 0.0) + jnp.log1p(small)


def silu(v):
    half = 0.5 * v
    return half + half * jnp.tanh(half)


def summary_kernel(
    mix_ref, halo_ref, step_ref, bias_ref, taps_ref, conv_bias_ref, decay_ref, writes_ref,
    rate_ref, signal_ref, msg_ref, ext, spread, *, block, taps
):
    decay = -jnp.exp(decay_ref[...]) * LOG2E

    @pl.when(pl.program_id(0) == 0)
    def _():
        for b in range(2):
            across = jnp.transpose(writes_ref[b].astype(F32))
            wide = jnp.concatenate([across] * NST, axis=1)
            state = lax.broadcasted_iota(jnp.int32, wide.shape, 0)
            owner = lax.broadcasted_iota(jnp.int32, wide.shape, 1) // block
            spread[b] = jnp.where(state == owner, wide, 0.0).astype(BF16)

    row = lax.broadcasted_iota(jnp.int32, (block, 2 * block), 0)
    col = lax.broadcasted_iota(jnp.int32, (block, 2 * block), 1) % block
    later = (col > row).astype(BF16)
    states, ends = [], []
    for b in range(2):
        ext[b, :8] = halo_ref[b]
        ext[b, 8:] = mix_ref[b].astype(F32)
        summed = conv_bias_ref[...]
        for m in range(taps):
            summed = summed + taps_ref[m:m + 1] * ext[b, pl.ds(8 - taps + 1 + m, block)]
        signal = silu(summed)
        rate = softplus(step_ref[b].astype(F32) + bias_ref[...])
        rate_ref[b] = rate
        signal_ref[b] = signal
        inflow = (rate * signal).astype(BF16)
        high = rate.astype(BF16)
        low = (rate - high.astype(F32)).astype(BF16)
        remaining = dot_nn(later, jnp.concatenate([high, low], axis=0))
        ends.append(remaining[:1] + rate[:1])
        state = 0.0
        for g in range(0, NST, 4):
            kept = [
                jnp.exp2(decay[n:n + 1] * remaining).astype(BF16) * inflow for n in range(g, g + 4)
            ]
            part = spread[b, :, g * block:(g + 4) * block]
            state = state + dot_nn(part, jnp.concatenate(kept, axis=0))
        states.append(state)
    rows = []
    for end in ends:
        high = end.astype(BF16).astype(F32)
        rows += [high, end - high]
    rows.append(jnp.zeros((8 - len(rows), rows[0].shape[1]), F32))
    message = jnp.concatenate(states + rows, axis=0).astype(BF16)
    for j in range(message.shape[1] // LANES):
        msg_ref[j] = message[:, j * LANES:(j + 1) * LANES]


def summarize(mix, halo, step, bias, taps, conv_bias, decay_log, writes):
    _, block, channels = mix.shape
    tile = min(WIDE, channels)
    seq = pl.BlockSpec((2, block, tile), lambda c: (0, 0, c))
    line = lambda rows: pl.BlockSpec((rows, tile), lambda c: (0, c))
    return pl.pallas_call(
        functools.partial(summary_kernel, block=block, taps=taps.shape[0]),
        grid=(channels // tile,),
        in_specs=[
            seq,
            pl.BlockSpec((2, 8, tile), lambda c: (0, 0, c)),
            seq,
            line(1),
            line(taps.shape[0]),
            line(1),
            line(NST),
            pl.BlockSpec(writes.shape, lambda c: (0, 0, 0)),
        ],
        out_specs=[seq, seq, pl.BlockSpec((tile // LANES, MSG_ROWS, LANES), lambda c: (c, 0, 0))],
        out_shape=[
            jax.ShapeDtypeStruct(mix.shape, F32),
            jax.ShapeDtypeStruct(mix.shape, F32),
            jax.ShapeDtypeStruct((channels // LANES, MSG_ROWS, LANES), BF16),
        ],
        scratch_shapes=[
            pltpu.VMEM((2, 8 + block, tile), F32),
            pltpu.VMEM((2, NST, NST * block), BF16),
        ],
        compiler_params=pltpu.CompilerParams(vmem_limit_bytes=VMEM),
        cost_estimate=pl.CostEstimate(flops=10**8, bytes_accessed=7 * 10**6, transcendentals=9 * 10**6),
        name="summarize",
    )(mix, halo, step, bias, taps, conv_bias, decay_log, writes)


def prefix_kernel(msg_ref, decay_ref, out_ref, *, pairs):
    decay = -jnp.exp(decay_ref[...]) * LOG2E

    def hop(j, state, half):
        out_ref[j, half * NST:(half + 1) * NST] = state.astype(BF16)
        piece = msg_ref[j].astype(F32)
        end = piece[2 * NST + 2 * half:2 * NST + 2 * half + 1] + piece[2 * NST + 2 * half + 1:2 * NST + 2 * half + 2]
        return jnp.exp2(decay * end) * state + piece[half * NST:(half + 1) * NST]

    state = jnp.zeros(decay.shape, F32)
    state = lax.fori_loop(0, pairs, lambda j, s: hop(j, s, 0), state, unroll=8)
    lax.fori_loop(0, pairs, lambda j, s: hop(pairs - 1 - j, s, 1), state, unroll=8)


def prefix(msg, decay_part):
    pairs = msg.shape[0]
    return pl.pallas_call(
        functools.partial(prefix_kernel, pairs=pairs),
        out_shape=jax.ShapeDtypeStruct((pairs, 2 * NST, LANES), BF16),
        cost_estimate=pl.CostEstimate(flops=10**6, bytes_accessed=6 * 10**5, transcendentals=10**5),
        name="prefix",
    )(msg, decay_part)


def scan_kernel(
    rate_ref, signal_ref, gate_ref, start_ref, decay_ref, skip_ref, writes_ref, reads_ref,
    out_ref, inflow, held, mats, wide, *, block
):
    tile = rate_ref.shape[2]
    cols = tile // LANES
    group = 16
    decay = -jnp.exp(decay_ref[...]) * LOG2E

    @pl.when(pl.program_id(0) == 0)
    def _():
        for b in range(2):
            across = jnp.transpose(writes_ref[b].astype(F32))
            for t in range(block):
                wide[b, t] = jnp.broadcast_to(across[:, t:t + 1], (NST, LANES))
            for g in range(block // group):
                rows = reads_ref[b, g * group:(g + 1) * group].astype(F32)
                spread = jnp.concatenate([rows] * group, axis=1)
                token = lax.broadcasted_iota(jnp.int32, spread.shape, 0)
                owner = lax.broadcasted_iota(jnp.int32, spread.shape, 1) // NST
                mats[b, g] = jnp.where(token == owner, spread, 0.0).astype(BF16)

    for b in range(2):
        inflow[b] = rate_ref[b] * signal_ref[b]

    def start(b):
        return jnp.concatenate(
            [start_ref[j, b * NST:(b + 1) * NST].astype(F32) for j in range(cols)], axis=1
        )

    def some(g, states):
        states = list(states)
        for k in range(group):
            t = g * group + k
            for b in range(2):
                kept = jnp.exp2(decay * rate_ref[b, pl.ds(t, 1)])
                write = jnp.concatenate([wide[b, t]] * cols, axis=1)
                states[b] = kept * states[b] + inflow[b, pl.ds(t, 1)] * write
                held[b, t * NST:(t + 1) * NST] = states[b].astype(BF16)
        at = g * group
        for b in range(2):
            summed = dot_nn(mats[b, g], held[b, at * NST:(at + group) * NST])
            mixed = summed + skip_ref[...] * signal_ref[b, pl.ds(at, group)]
            gate = gate_ref[b, pl.ds(at, group)].astype(F32)
            out_ref[b, pl.ds(at, group)] = (mixed * silu(gate)).astype(BF16)
        return tuple(states)

    states = (start(0), start(1))
    for g in range(block // group):
        states = some(g, states)


def scan(rate, signal, gate, start, decay_log, skip, writes, reads):
    _, block, channels = rate.shape
    tile = min(TILE, channels)
    seq = pl.BlockSpec((2, block, tile), lambda c: (0, 0, c))
    line = lambda rows: pl.BlockSpec((rows, tile), lambda c: (0, c))
    return pl.pallas_call(
        functools.partial(scan_kernel, block=block),
        grid=(channels // tile,),
        in_specs=[
            seq,
            seq,
            seq,
            pl.BlockSpec((tile // LANES, 2 * NST, LANES), lambda c: (c, 0, 0)),
            line(NST),
            line(1),
            pl.BlockSpec(writes.shape, lambda c: (0, 0, 0)),
            pl.BlockSpec(reads.shape, lambda c: (0, 0, 0)),
        ],
        out_specs=seq,
        out_shape=jax.ShapeDtypeStruct(gate.shape, BF16),
        scratch_shapes=[
            pltpu.VMEM((2, block, tile), F32),
            pltpu.VMEM((2, block * NST, tile), BF16),
            pltpu.VMEM((2, block // 16, 16, 16 * NST), BF16),
            pltpu.VMEM((2, block, NST, LANES), F32),
        ],
        compiler_params=pltpu.CompilerParams(vmem_limit_bytes=VMEM),
        cost_estimate=pl.CostEstimate(flops=10**8, bytes_accessed=8 * 10**6, transcendentals=9 * 10**6),
        name="scan",
    )(rate, signal, gate, start, decay_log, skip, writes, reads)


def body(
    queries,
    projected_key_rows,
    values,
    mixer_input,
    step_raw,
    gate_input,
    state_write,
    state_read,
    decay_log,
    step_bias,
    conv_weight,
    conv_bias,
    skip_gain,
):
    rank = lax.axis_index("ctx")
    count = lax.axis_size("ctx")
    block = queries.shape[2]
    taps = conv_weight.shape[0]

    halves = mixer_input[0]
    tails = halves[:, block - (taps - 1):]
    forward = [(i, i + 1) for i in range(count - 1)]
    backward = [(i + 1, i) for i in range(count - 1)]
    before_first = lax.ppermute(tails[0], "ctx", forward)
    before_second = lax.ppermute(tails[1], "ctx", backward)

    row, place = rank // ROW, rank % ROW
    core, odd = lax.axis_index("dp") % 2, row % 2
    swaps = [[], []]
    for k in range(2):
        for dp in range(lax.axis_size("dp")):
            for ctx in range(count):
                x, z = ctx // ROW, ctx % ROW
                target = (dp // 2 * 2 + x // 2) * count + (dp % 2 * 2 + (x % 2 ^ k)) * ROW + z
                swaps[k].append((dp * count + ctx, target))
    def along(hop):
        return [(i, i // ROW * ROW + (i + hop) % ROW) for i in range(count)]

    cores = [(i, i ^ 1) for i in range(lax.axis_size("dp"))]

    def swap(array):
        width = array.shape[-1] // 2
        low, high = array[..., :width], array[..., width:]
        parts = [jnp.where(odd == k, low, high) for k in range(2)]
        return [lax.ppermute(part, ("dp", "ctx"), pairs) for part, pairs in zip(parts, swaps)]

    def swap_back(k, array):
        return lax.ppermute(array, ("dp", "ctx"), [(t, f) for f, t in swaps[k]])

    parts = split(jnp.reshape(odd, (1,)).astype(jnp.int32), projected_key_rows[0], values[0])
    parts = [lax.ppermute(part, ("dp", "ctx"), pairs) for part, pairs in zip(parts, swaps)]
    last = jnp.reshape(rank == count - 1, (1,)).astype(jnp.int32)
    kv, halo = pack(last, parts[0], parts[1], before_first, before_second, tails[0])
    near = [lax.ppermute(kv, "ctx", along(-k)) for k in (1, 2, -1, -2)]
    asked = swap(queries[0])

    rate, signal, msg = summarize(
        halves, halo, step_raw[0], step_bias[None], conv_weight, conv_bias[None], decay_log, state_write[0]
    )
    one, two, back_one, back_two = after(near, rate)
    (msg,) = after([msg], one)
    three = lax.ppermute(two, "ctx", along(-1))
    back_three = lax.ppermute(back_two, "ctx", along(1))
    four = lax.ppermute(two, "ctx", along(-2))
    msg = lax.all_to_all(msg, "ctx", 0, 0, tiled=True)
    kv_own = assemble(
        jnp.reshape(place, (1,)).astype(jnp.int32),
        [kv, one, two, three, four, back_three, back_two, back_one],
        msg,
    )
    kv_other = lax.ppermute(kv_own, "dp", cores)
    decay_part = lax.dynamic_slice_in_dim(decay_log, rank * LANES, LANES, 1)
    start = lax.all_to_all(prefix(msg, decay_part), "ctx", 0, 0, tiled=True)
    selected = scan(
        rate, signal, gate_input[0], start, decay_log, skip_gain[None], state_write[0], state_read[0]
    )
    answers = []
    for k in range(2):
        where = jnp.stack([2 * core + (odd + k) % 2, place, odd, core]).astype(jnp.int32)
        answers.append(swap_back(k, attend(where, asked[k], kv_own, kv_other)))
    low = jnp.where(odd == 0, answers[0], answers[1])
    high = jnp.where(odd == 0, answers[1], answers[0])
    attended = jnp.concatenate([low, high], axis=-1)
    return (attended[None], selected[None])


def solution(mesh):
    rows = P(("dp", "ctx"), None, None, "tp")
    shared = P(("dp", "ctx"), None, None, None)
    return jax.shard_map(
        body,
        mesh=mesh,
        in_specs=(rows,) * 6 + (shared,) * 2
        + (P(None, "tp"), P("tp"), P(None, "tp"), P("tp"), P("tp")),
        out_specs=(rows, rows),
        check_vma=False,
    )
```

```python
import functools

import jax
import jax.numpy as jnp
from jax import lax
from jax.experimental import pallas as pl
from jax.experimental.pallas import tpu as pltpu
from jax.sharding import PartitionSpec as P

HEAD = 128
NST = 16
LOG2E = 1.4426950408889634
TILE = 512
WIDE = 1024
LANES = 128
MSG_ROWS = 40
ROW = 8
BIG_NEG = -1e30
VMEM = 56 * 2**20
F32 = jnp.float32
BF16 = jnp.bfloat16


def dot_nt(a, b):
    return lax.dot_general(a, b, (((1,), (1,)), ((), ())), preferred_element_type=F32)


def dot_nn(a, b):
    return lax.dot_general(a, b, (((1,), (0,)), ((), ())), preferred_element_type=F32)


def attend_kernel(where_ref, q_ref, kv_ref, o_ref, qs, acc, top, kvs, sems, *, block, heads, turns, turn):
    mine, place, odd = where_ref[turn], where_ref[2], where_ref[3]
    rows = heads * block
    span = ROW * block
    scale = LOG2E * HEAD ** -0.5

    def fetch(row):
        source = kv_ref.at[pl.ds((row // 2) * ROW, ROW), (row + odd) % 2]
        return pltpu.make_async_copy(source, kvs.at[row], sems.at[row])

    for d in range(turns):
        fetch((mine + d) % turns).start()

    for b in range(2):
        for h in range(heads):
            scaled = q_ref[b, :, h * HEAD:(h + 1) * HEAD].astype(F32) * scale
            high = scaled.astype(BF16)
            low = (scaled - high.astype(F32)).astype(BF16)
            qs[pl.ds(b * rows + h * block, block), :HEAD] = high
            qs[pl.ds(b * rows + h * block, block), HEAD:] = low

    def score(b, row, half):
        keys = kvs[row, :, 0, half].reshape(span, HEAD)
        at = pl.multiple_of(b * rows, rows)
        return dot_nt(qs[pl.ds(at, rows)], jnp.concatenate([keys, keys], axis=1))

    def update(b, row, half, scores, first):
        vals = kvs[row, :, 1, half].reshape(span, HEAD)
        at = pl.multiple_of(b * rows, rows)
        best = jnp.broadcast_to(jnp.max(scores, axis=1, keepdims=True), (rows, LANES))
        if not first:
            old = top[pl.ds(at, rows)]
            best = jnp.maximum(best, old)
        weights = jnp.exp2(scores - jnp.concatenate([best] * (span // LANES), axis=1)).astype(BF16)
        added = dot_nn(weights, jnp.concatenate([vals, jnp.ones_like(vals)], axis=1))
        if not first:
            factor = jnp.exp2(old - best)
            added = added + acc[pl.ds(at, rows)] * jnp.concatenate([factor, factor], axis=1)
        acc[pl.ds(at, rows)] = added
        top[pl.ds(at, rows)] = best

    token = lax.broadcasted_iota(jnp.int32, (rows, span), 0) % block
    key = lax.broadcasted_iota(jnp.int32, (rows, span), 1)
    upto = key <= token + place * block
    after = (key >= (place + 1) * block) | ((key >= place * block) & upto)

    fetch(mine).wait()
    early = score(0, mine, 0)
    late = score(1, mine, 0)
    own = score(1, mine, 1)
    update(0, mine, 0, jnp.where(upto, early, BIG_NEG), True)
    update(1, mine, 0, late, True)
    update(1, mine, 1, jnp.where(after, own, BIG_NEG), False)

    def other(d, carry):
        row = (mine + d) % turns
        later = (row > mine).astype(jnp.int32)
        fetch(row).wait()
        late = score(1, row, 0)
        second = score(later, row, later)
        update(1, row, 0, late, False)
        update(later, row, later, second, False)
        return carry

    lax.fori_loop(1, turns, other, 0)
    for b in range(2):
        for h in range(heads):
            done = acc[pl.ds(b * rows + h * block, block)]
            o_ref[b, :, h * HEAD:(h + 1) * HEAD] = (done[:, :HEAD] / done[:, HEAD:]).astype(BF16)


def attend(where, turn, queries, kv):
    _, block, width = queries.shape
    heads = width // HEAD
    turns = 2 * kv.shape[0] // ROW
    return pl.pallas_call(
        functools.partial(attend_kernel, block=block, heads=heads, turns=turns, turn=turn),
        in_specs=[
            pl.BlockSpec(memory_space=pltpu.SMEM),
            pl.BlockSpec(memory_space=pltpu.VMEM),
            pl.BlockSpec(memory_space=pl.ANY),
        ],
        out_specs=pl.BlockSpec(memory_space=pltpu.VMEM),
        scratch_shapes=[
            pltpu.VMEM((2 * heads * block, 2 * HEAD), BF16),
            pltpu.VMEM((2 * heads * block, 2 * HEAD), F32),
            pltpu.VMEM((2 * heads * block, LANES), F32),
            pltpu.VMEM((turns, ROW, 2, 2, block, HEAD), BF16),
            pltpu.SemaphoreType.DMA((turns,)),
        ],
        out_shape=jax.ShapeDtypeStruct(queries.shape, BF16),
        compiler_params=pltpu.CompilerParams(vmem_limit_bytes=24 * 2**20),
        cost_estimate=pl.CostEstimate(flops=10**9, bytes_accessed=3 * 10**6, transcendentals=3 * 10**6),
        name="attend",
    )(where, queries, kv)


def split_kernel(odd_ref, keys_ref, values_ref, first_ref, second_ref):
    odd = odd_ref[3]
    for k, out in enumerate((first_ref, second_ref)):
        at = pl.multiple_of(((odd + k) % 2) * HEAD, HEAD)
        out[0] = keys_ref[:, :, pl.ds(at, HEAD)]
        out[1] = values_ref[:, :, pl.ds(at, HEAD)]


def split(odd, keys, values):
    half, block, _ = keys.shape
    part = jax.ShapeDtypeStruct((2, half, block, HEAD), BF16)
    return pl.pallas_call(
        split_kernel,
        in_specs=[pl.BlockSpec(memory_space=pltpu.SMEM)] + [pl.BlockSpec(memory_space=pltpu.VMEM)] * 2,
        out_specs=[pl.BlockSpec(memory_space=pltpu.VMEM)] * 2,
        out_shape=[part, part],
        name="split",
    )(odd, keys, values)


def pack_kernel(first_ref, second_ref, before_ref, after_ref, pair_ref):
    del before_ref, after_ref
    pair_ref[0] = first_ref[...]
    pair_ref[1] = second_ref[...]


def pack(first, second, before, after):
    vmem = pl.BlockSpec(memory_space=pltpu.VMEM)
    anywhere = pl.BlockSpec(memory_space=pl.ANY)
    return pl.pallas_call(
        pack_kernel,
        in_specs=[vmem] * 2 + [anywhere] * 2,
        out_specs=vmem,
        out_shape=jax.ShapeDtypeStruct((2,) + first.shape, BF16),
        name="pack",
    )(first, second, before, after)


def softplus(v):
    small = jnp.exp(-jnp.abs(v))
    return jnp.maximum(v, 0.0) + jnp.log1p(small)


def silu(v):
    half = 0.5 * v
    return half + half * jnp.tanh(half)


def summary_kernel(
    info_ref, before_ref, after_ref, tail_ref, mix_ref, step_ref, bias_ref, taps_ref, conv_bias_ref, decay_ref, writes_ref,
    rate_ref, signal_ref, msg_ref, ext, spread, *, block, taps
):
    decay = -jnp.exp(decay_ref[...]) * LOG2E

    @pl.when(pl.program_id(0) == 0)
    def _():
        for b in range(2):
            across = writes_ref[b].astype(F32)
            wide = jnp.concatenate([across] * NST, axis=1)
            state = lax.broadcasted_iota(jnp.int32, wide.shape, 0)
            owner = lax.broadcasted_iota(jnp.int32, wide.shape, 1) // block
            spread[b] = jnp.where(state == owner, wide, 0.0).astype(BF16)

    row = lax.broadcasted_iota(jnp.int32, (block, 2 * block), 0)
    col = lax.broadcasted_iota(jnp.int32, (block, 2 * block), 1) % block
    later = (col > row).astype(BF16)
    follow = jnp.where(info_ref[6] == 1, tail_ref[...].astype(F32), after_ref[...].astype(F32))
    halos = (before_ref[...].astype(F32), follow)
    states, ends = [], []
    for b in range(2):
        ext[b, 8 - taps + 1:8] = halos[b]
        ext[b, 8:] = mix_ref[b].astype(F32)
        summed = conv_bias_ref[...]
        for m in range(taps):
            summed = summed + taps_ref[m:m + 1] * ext[b, pl.ds(8 - taps + 1 + m, block)]
        signal = silu(summed)
        rate = softplus(step_ref[b].astype(F32) + bias_ref[...])
        rate_ref[b] = rate
        signal_ref[b] = signal
        inflow = (rate * signal).astype(BF16)
        high = rate.astype(BF16)
        low = (rate - high.astype(F32)).astype(BF16)
        remaining = dot_nn(later, jnp.concatenate([high, low], axis=0))
        ends.append(remaining[:1] + rate[:1])
        state = 0.0
        for g in range(0, NST, 4):
            kept = [
                jnp.exp2(decay[n:n + 1] * remaining).astype(BF16) * inflow for n in range(g, g + 4)
            ]
            part = spread[b, :, g * block:(g + 4) * block]
            state = state + dot_nn(part, jnp.concatenate(kept, axis=0))
        states.append(state)
    rows = []
    for end in ends:
        high = end.astype(BF16).astype(F32)
        rows += [high, end - high]
    rows.append(jnp.zeros((8 - len(rows), rows[0].shape[1]), F32))
    message = jnp.concatenate(states + rows, axis=0).astype(BF16)
    for j in range(message.shape[1] // LANES):
        msg_ref[j] = message[:, j * LANES:(j + 1) * LANES]


def summarize(info, before, after, tail, mix, step, bias, taps, conv_bias, decay_log, writes):
    _, block, channels = mix.shape
    tile = min(WIDE, channels)
    seq = pl.BlockSpec((2, block, tile), lambda c: (0, 0, c))
    line = lambda rows: pl.BlockSpec((rows, tile), lambda c: (0, c))
    return pl.pallas_call(
        functools.partial(summary_kernel, block=block, taps=taps.shape[0]),
        grid=(channels // tile,),
        in_specs=[
            pl.BlockSpec(memory_space=pltpu.SMEM),
            line(before.shape[0]),
            line(before.shape[0]),
            line(before.shape[0]),
            seq,
            seq,
            line(1),
            line(taps.shape[0]),
            line(1),
            line(NST),
            pl.BlockSpec(writes.shape, lambda c: (0, 0, 0)),
        ],
        out_specs=[seq, seq, pl.BlockSpec((tile // LANES, MSG_ROWS, LANES), lambda c: (c, 0, 0))],
        out_shape=[
            jax.ShapeDtypeStruct(mix.shape, F32),
            jax.ShapeDtypeStruct(mix.shape, F32),
            jax.ShapeDtypeStruct((channels // LANES, MSG_ROWS, LANES), BF16),
        ],
        scratch_shapes=[
            pltpu.VMEM((2, 8 + block, tile), F32),
            pltpu.VMEM((2, NST, NST * block), BF16),
        ],
        compiler_params=pltpu.CompilerParams(vmem_limit_bytes=VMEM),
        cost_estimate=pl.CostEstimate(flops=10**8, bytes_accessed=7 * 10**6, transcendentals=9 * 10**6),
        name="summarize",
    )(info, before, after, tail, mix, step, bias, taps, conv_bias, decay_log, writes)


def prefix_kernel(info_ref, msg_ref, decay_ref, out_ref, *, pairs):
    del info_ref
    decay = -jnp.exp(decay_ref[...]) * LOG2E

    def hop(j, state, half):
        out_ref[j, half * NST:(half + 1) * NST] = state.astype(BF16)
        piece = msg_ref[j].astype(F32)
        end = piece[2 * NST + 2 * half:2 * NST + 2 * half + 1] + piece[2 * NST + 2 * half + 1:2 * NST + 2 * half + 2]
        return jnp.exp2(decay * end) * state + piece[half * NST:(half + 1) * NST]

    state = jnp.zeros(decay.shape, F32)
    state = lax.fori_loop(0, pairs, lambda j, s: hop(j, s, 0), state, unroll=8)
    lax.fori_loop(0, pairs, lambda j, s: hop(pairs - 1 - j, s, 1), state, unroll=8)


def prefix(info, msg, decay_log):
    pairs = msg.shape[0]
    return pl.pallas_call(
        functools.partial(prefix_kernel, pairs=pairs),
        grid_spec=pltpu.PrefetchScalarGridSpec(
            num_scalar_prefetch=1,
            grid=(1,),
            in_specs=[
                pl.BlockSpec(msg.shape, lambda i, info: (0, 0, 0)),
                pl.BlockSpec((NST, LANES), lambda i, info: (0, info[5])),
            ],
            out_specs=pl.BlockSpec((pairs, 2 * NST, LANES), lambda i, info: (0, 0, 0)),
        ),
        out_shape=jax.ShapeDtypeStruct((pairs, 2 * NST, LANES), BF16),
        cost_estimate=pl.CostEstimate(flops=10**6, bytes_accessed=6 * 10**5, transcendentals=10**5),
        name="prefix",
    )(info, msg, decay_log)


def scan_kernel(
    rate_ref, signal_ref, gate_ref, start_ref, decay_ref, skip_ref, writes_ref, reads_ref,
    out_ref, inflow, held, mats, wide, *, block
):
    tile = rate_ref.shape[2]
    cols = tile // LANES
    group = 16
    decay = -jnp.exp(decay_ref[...]) * LOG2E

    @pl.when(pl.program_id(0) == 0)
    def _():
        for b in range(2):
            across = writes_ref[b].astype(F32)
            turned = jnp.transpose(reads_ref[b].astype(F32))
            for t in range(block):
                wide[b, t] = jnp.broadcast_to(across[:, t:t + 1], (NST, LANES))
            for g in range(block // group):
                rows = turned[g * group:(g + 1) * group]
                spread = jnp.concatenate([rows] * group, axis=1)
                token = lax.broadcasted_iota(jnp.int32, spread.shape, 0)
                owner = lax.broadcasted_iota(jnp.int32, spread.shape, 1) // NST
                mats[b, g] = jnp.where(token == owner, spread, 0.0).astype(BF16)

    for b in range(2):
        inflow[b] = rate_ref[b] * signal_ref[b]

    def start(b):
        return jnp.concatenate(
            [start_ref[j, b * NST:(b + 1) * NST].astype(F32) for j in range(cols)], axis=1
        )

    def some(g, states):
        states = list(states)
        for k in range(group):
            t = g * group + k
            for b in range(2):
                kept = jnp.exp2(decay * rate_ref[b, pl.ds(t, 1)])
                write = jnp.concatenate([wide[b, t]] * cols, axis=1)
                states[b] = kept * states[b] + inflow[b, pl.ds(t, 1)] * write
                held[b, t * NST:(t + 1) * NST] = states[b].astype(BF16)
        at = g * group
        for b in range(2):
            summed = dot_nn(mats[b, g], held[b, at * NST:(at + group) * NST])
            mixed = summed + skip_ref[...] * signal_ref[b, pl.ds(at, group)]
            gate = gate_ref[b, pl.ds(at, group)].astype(F32)
            out_ref[b, pl.ds(at, group)] = (mixed * silu(gate)).astype(BF16)
        return tuple(states)

    states = (start(0), start(1))
    for g in range(block // group):
        states = some(g, states)


def scan(rate, signal, gate, start, decay_log, skip, writes, reads):
    _, block, channels = rate.shape
    tile = min(TILE, channels)
    seq = pl.BlockSpec((2, block, tile), lambda c: (0, 0, c))
    line = lambda rows: pl.BlockSpec((rows, tile), lambda c: (0, c))
    return pl.pallas_call(
        functools.partial(scan_kernel, block=block),
        grid=(channels // tile,),
        in_specs=[
            seq,
            seq,
            seq,
            pl.BlockSpec((tile // LANES, 2 * NST, LANES), lambda c: (c, 0, 0)),
            line(NST),
            line(1),
            pl.BlockSpec(writes.shape, lambda c: (0, 0, 0)),
            pl.BlockSpec(reads.shape, lambda c: (0, 0, 0)),
        ],
        out_specs=seq,
        out_shape=jax.ShapeDtypeStruct(gate.shape, BF16),
        scratch_shapes=[
            pltpu.VMEM((2, block, tile), F32),
            pltpu.VMEM((2, block * NST, tile), BF16),
            pltpu.VMEM((2, block // 16, 16, 16 * NST), BF16),
            pltpu.VMEM((2, block, NST, LANES), F32),
        ],
        compiler_params=pltpu.CompilerParams(vmem_limit_bytes=VMEM),
        cost_estimate=pl.CostEstimate(flops=10**8, bytes_accessed=8 * 10**6, transcendentals=9 * 10**6),
        name="scan",
    )(rate, signal, gate, start, decay_log, skip, writes, reads)


def body(
    queries,
    projected_key_rows,
    values,
    mixer_input,
    step_raw,
    gate_input,
    state_write,
    state_read,
    decay_log,
    step_bias,
    conv_weight,
    conv_bias,
    skip_gain,
):
    rank = lax.axis_index("ctx")
    count = lax.axis_size("ctx")
    block = queries.shape[2]
    taps = conv_weight.shape[0]

    halves = mixer_input[0]
    tails = halves[:, block - (taps - 1):]
    forward = [(i, i + 1) for i in range(count - 1)]
    backward = [(i + 1, i) for i in range(count - 1)]
    before_first = lax.ppermute(tails[0], "ctx", forward)
    before_second = lax.ppermute(tails[1], "ctx", backward)

    row, place = rank // ROW, rank % ROW
    core, odd = lax.axis_index("dp") % 2, row % 2
    info = jnp.stack(
        [2 * core + odd, 2 * core + 1 - odd, place, odd, core, rank, (rank == count - 1).astype(rank.dtype)]
    ).astype(jnp.int32)
    swaps = [[], []]
    for k in range(2):
        for dp in range(lax.axis_size("dp")):
            for ctx in range(count):
                x, z = ctx // ROW, ctx % ROW
                target = (dp // 2 * 2 + x // 2) * count + (dp % 2 * 2 + (x % 2 ^ k)) * ROW + z
                swaps[k].append((dp * count + ctx, target))
    gathers = [
        [(pair * 2 + c) * count + x * ROW + z for c in range(2) for z in range(ROW)]
        for pair in range(lax.axis_size("dp") // 2)
        for x in range(count // ROW)
    ]

    def swap(array):
        width = array.shape[-1] // 2
        low, high = array[..., :width], array[..., width:]
        parts = [jnp.where(odd == k, low, high) for k in range(2)]
        return [lax.ppermute(part, ("dp", "ctx"), pairs) for part, pairs in zip(parts, swaps)]

    def swap_back(k, array):
        return lax.ppermute(array, ("dp", "ctx"), [(t, f) for f, t in swaps[k]])

    parts = split(info, projected_key_rows[0], values[0])
    parts = [lax.ppermute(part, ("dp", "ctx"), pairs) for part, pairs in zip(parts, swaps)]
    kv = pack(*parts, before_first, before_second)
    kv = lax.all_gather(kv, ("dp", "ctx"), axis_index_groups=gathers)
    asked = swap(queries[0])

    write = jnp.swapaxes(state_write[0], 1, 2)
    read = jnp.swapaxes(state_read[0], 1, 2)
    rate, signal, msg = summarize(
        info, before_first, before_second, tails[0], halves, step_raw[0], step_bias[None], conv_weight,
        conv_bias[None], decay_log, write,
    )
    msg = lax.all_to_all(msg, "ctx", 0, 0, tiled=True)
    start = prefix(info, msg, decay_log)
    start = lax.all_to_all(start, "ctx", 0, 0, tiled=True)
    selected = scan(rate, signal, gate_input[0], start, decay_log, skip_gain[None], write, read)
    answers = []
    for k in range(2):
        answers.append(swap_back(k, attend(info, k, asked[k], kv)))
    low = jnp.where(odd == 0, answers[0], answers[1])
    high = jnp.where(odd == 0, answers[1], answers[0])
    attended = jnp.concatenate([low, high], axis=-1)
    return (attended[None], selected[None])


def solution(mesh):
    rows = P(("dp", "ctx"), None, None, "tp")
    shared = P(("dp", "ctx"), None, None, None)
    return jax.shard_map(
        body,
        mesh=mesh,
        in_specs=(rows,) * 6 + (shared,) * 2
        + (P(None, "tp"), P("tp"), P(None, "tp"), P("tp"), P("tp")),
        out_specs=(rows, rows),
        check_vma=False,
    )
```

```python
import functools

import jax
import jax.numpy as jnp
from jax import lax
from jax.experimental import pallas as pl
from jax.experimental.pallas import tpu as pltpu
from jax.sharding import PartitionSpec as P

HEAD = 128
NST = 16
LOG2E = 1.4426950408889634
TILE = 512
WIDE = 1024
LANES = 128
MSG_ROWS = 40
ROW = 8
BIG_NEG = -1e30
VMEM = 56 * 2**20
SMALL = 8 * 2**20
F32 = jnp.float32
BF16 = jnp.bfloat16


def dot_nt(a, b):
    return lax.dot_general(a, b, (((1,), (1,)), ((), ())), preferred_element_type=F32)


def dot_nn(a, b):
    return lax.dot_general(a, b, (((1,), (0,)), ((), ())), preferred_element_type=F32)


def attend_kernel(where_ref, q_ref, kv_ref, o_ref, qs, acc, top, kvs, sems, *, block, heads, turns, turn):
    mine, place, odd = where_ref[turn], where_ref[2], where_ref[3]
    rows = heads * block
    span = ROW * block
    scale = LOG2E * HEAD ** -0.5

    def fetch(row):
        source = kv_ref.at[pl.ds((row // 2) * ROW, ROW), (row + odd) % 2]
        return pltpu.make_async_copy(source, kvs.at[row], sems.at[row])

    for d in range(turns):
        fetch((mine + d) % turns).start()

    for b in range(2):
        for h in range(heads):
            scaled = q_ref[b, :, h * HEAD:(h + 1) * HEAD].astype(F32) * scale
            high = scaled.astype(BF16)
            low = (scaled - high.astype(F32)).astype(BF16)
            qs[pl.ds(b * rows + h * block, block), :HEAD] = high
            qs[pl.ds(b * rows + h * block, block), HEAD:] = low

    def score(b, row, half):
        keys = kvs[row, :, 0, half].reshape(span, HEAD)
        at = pl.multiple_of(b * rows, rows)
        return dot_nt(qs[pl.ds(at, rows)], jnp.concatenate([keys, keys], axis=1))

    def update(b, row, half, scores, first):
        vals = kvs[row, :, 1, half].reshape(span, HEAD)
        at = pl.multiple_of(b * rows, rows)
        best = jnp.broadcast_to(jnp.max(scores, axis=1, keepdims=True), (rows, LANES))
        if not first:
            old = top[pl.ds(at, rows)]
            best = jnp.maximum(best, old)
        weights = jnp.exp2(scores - jnp.concatenate([best] * (span // LANES), axis=1)).astype(BF16)
        added = dot_nn(weights, jnp.concatenate([vals, jnp.ones_like(vals)], axis=1))
        if not first:
            factor = jnp.exp2(old - best)
            added = added + acc[pl.ds(at, rows)] * jnp.concatenate([factor, factor], axis=1)
        acc[pl.ds(at, rows)] = added
        top[pl.ds(at, rows)] = best

    token = lax.broadcasted_iota(jnp.int32, (rows, span), 0) % block
    key = lax.broadcasted_iota(jnp.int32, (rows, span), 1)
    upto = key <= token + place * block
    after = (key >= (place + 1) * block) | ((key >= place * block) & upto)

    fetch(mine).wait()
    early = score(0, mine, 0)
    late = score(1, mine, 0)
    own = score(1, mine, 1)
    update(0, mine, 0, jnp.where(upto, early, BIG_NEG), True)
    update(1, mine, 0, late, True)
    update(1, mine, 1, jnp.where(after, own, BIG_NEG), False)

    def other(d, carry):
        row = (mine + d) % turns
        later = (row > mine).astype(jnp.int32)
        fetch(row).wait()
        late = score(1, row, 0)
        second = score(later, row, later)
        update(1, row, 0, late, False)
        update(later, row, later, second, False)
        return carry

    lax.fori_loop(1, turns, other, 0)
    for b in range(2):
        for h in range(heads):
            done = acc[pl.ds(b * rows + h * block, block)]
            o_ref[b, :, h * HEAD:(h + 1) * HEAD] = (done[:, :HEAD] / done[:, HEAD:]).astype(BF16)


def attend(where, turn, queries, kv):
    _, block, width = queries.shape
    heads = width // HEAD
    turns = 2 * kv.shape[0] // ROW
    return pl.pallas_call(
        functools.partial(attend_kernel, block=block, heads=heads, turns=turns, turn=turn),
        in_specs=[
            pl.BlockSpec(memory_space=pltpu.SMEM),
            pl.BlockSpec(memory_space=pltpu.VMEM),
            pl.BlockSpec(memory_space=pl.ANY),
        ],
        out_specs=pl.BlockSpec(memory_space=pltpu.VMEM),
        scratch_shapes=[
            pltpu.VMEM((2 * heads * block, 2 * HEAD), BF16),
            pltpu.VMEM((2 * heads * block, 2 * HEAD), F32),
            pltpu.VMEM((2 * heads * block, LANES), F32),
            pltpu.VMEM((turns, ROW, 2, 2, block, HEAD), BF16),
            pltpu.SemaphoreType.DMA((turns,)),
        ],
        out_shape=jax.ShapeDtypeStruct(queries.shape, BF16),
        compiler_params=pltpu.CompilerParams(vmem_limit_bytes=24 * 2**20),
        cost_estimate=pl.CostEstimate(flops=10**9, bytes_accessed=3 * 10**6, transcendentals=3 * 10**6),
        name="attend",
    )(where, queries, kv)


def split_kernel(odd_ref, keys_ref, values_ref, first_ref, second_ref):
    odd = odd_ref[3]
    for k, out in enumerate((first_ref, second_ref)):
        at = pl.multiple_of(((odd + k) % 2) * HEAD, HEAD)
        out[0] = keys_ref[:, :, pl.ds(at, HEAD)]
        out[1] = values_ref[:, :, pl.ds(at, HEAD)]


def split(odd, keys, values):
    half, block, _ = keys.shape
    part = jax.ShapeDtypeStruct((2, half, block, HEAD), BF16)
    return pl.pallas_call(
        split_kernel,
        in_specs=[pl.BlockSpec(memory_space=pltpu.SMEM)] + [pl.BlockSpec(memory_space=pltpu.VMEM)] * 2,
        out_specs=[pl.BlockSpec(memory_space=pltpu.VMEM)] * 2,
        out_shape=[part, part],
        compiler_params=pltpu.CompilerParams(vmem_limit_bytes=SMALL),
        name="split",
    )(odd, keys, values)


def pack_kernel(first_ref, second_ref, before_ref, after_ref, pair_ref):
    del before_ref, after_ref
    pair_ref[0] = first_ref[...]
    pair_ref[1] = second_ref[...]


def pack(first, second, before, after):
    vmem = pl.BlockSpec(memory_space=pltpu.VMEM)
    anywhere = pl.BlockSpec(memory_space=pl.ANY)
    return pl.pallas_call(
        pack_kernel,
        in_specs=[vmem] * 2 + [anywhere] * 2,
        out_specs=vmem,
        out_shape=jax.ShapeDtypeStruct((2,) + first.shape, BF16),
        compiler_params=pltpu.CompilerParams(vmem_limit_bytes=SMALL),
        name="pack",
    )(first, second, before, after)


def softplus(v):
    small = jnp.exp(-jnp.abs(v))
    return jnp.maximum(v, 0.0) + jnp.log1p(small)


def silu(v):
    half = 0.5 * v
    return half + half * jnp.tanh(half)


def summary_kernel(
    info_ref, before_ref, after_ref, tail_ref, mix_ref, step_ref, bias_ref, taps_ref, conv_bias_ref, decay_ref, writes_ref,
    rate_ref, signal_ref, msg_ref, ext, spread, *, block, taps
):
    decay = -jnp.exp(decay_ref[...]) * LOG2E

    @pl.when(pl.program_id(0) == 0)
    def _():
        for b in range(2):
            across = writes_ref[b].astype(F32)
            wide = jnp.concatenate([across] * NST, axis=1)
            state = lax.broadcasted_iota(jnp.int32, wide.shape, 0)
            owner = lax.broadcasted_iota(jnp.int32, wide.shape, 1) // block
            spread[b] = jnp.where(state == owner, wide, 0.0).astype(BF16)

    row = lax.broadcasted_iota(jnp.int32, (block, 2 * block), 0)
    col = lax.broadcasted_iota(jnp.int32, (block, 2 * block), 1) % block
    later = (col > row).astype(BF16)
    follow = jnp.where(info_ref[6] == 1, tail_ref[...].astype(F32), after_ref[...].astype(F32))
    halos = (before_ref[...].astype(F32), follow)
    states, ends = [], []
    for b in range(2):
        ext[b, 8 - taps + 1:8] = halos[b]
        ext[b, 8:] = mix_ref[b].astype(F32)
        summed = conv_bias_ref[...]
        for m in range(taps):
            summed = summed + taps_ref[m:m + 1] * ext[b, pl.ds(8 - taps + 1 + m, block)]
        signal = silu(summed)
        rate = softplus(step_ref[b].astype(F32) + bias_ref[...])
        rate_ref[b] = rate
        signal_ref[b] = signal
        inflow = (rate * signal).astype(BF16)
        high = rate.astype(BF16)
        low = (rate - high.astype(F32)).astype(BF16)
        remaining = dot_nn(later, jnp.concatenate([high, low], axis=0))
        ends.append(remaining[:1] + rate[:1])
        state = 0.0
        for g in range(0, NST, 4):
            kept = [
                jnp.exp2(decay[n:n + 1] * remaining).astype(BF16) * inflow for n in range(g, g + 4)
            ]
            part = spread[b, :, g * block:(g + 4) * block]
            state = state + dot_nn(part, jnp.concatenate(kept, axis=0))
        states.append(state)
    rows = []
    for end in ends:
        high = end.astype(BF16).astype(F32)
        rows += [high, end - high]
    rows.append(jnp.zeros((8 - len(rows), rows[0].shape[1]), F32))
    message = jnp.concatenate(states + rows, axis=0).astype(BF16)
    for j in range(message.shape[1] // LANES):
        msg_ref[j] = message[:, j * LANES:(j + 1) * LANES]


def summarize(info, before, after, tail, mix, step, bias, taps, conv_bias, decay_log, writes):
    _, block, channels = mix.shape
    tile = min(WIDE, channels)
    seq = pl.BlockSpec((2, block, tile), lambda c: (0, 0, c))
    line = lambda rows: pl.BlockSpec((rows, tile), lambda c: (0, c))
    return pl.pallas_call(
        functools.partial(summary_kernel, block=block, taps=taps.shape[0]),
        grid=(channels // tile,),
        in_specs=[
            pl.BlockSpec(memory_space=pltpu.SMEM),
            line(before.shape[0]),
            line(before.shape[0]),
            line(before.shape[0]),
            seq,
            seq,
            line(1),
            line(taps.shape[0]),
            line(1),
            line(NST),
            pl.BlockSpec(writes.shape, lambda c: (0, 0, 0)),
        ],
        out_specs=[seq, seq, pl.BlockSpec((tile // LANES, MSG_ROWS, LANES), lambda c: (c, 0, 0))],
        out_shape=[
            jax.ShapeDtypeStruct(mix.shape, F32),
            jax.ShapeDtypeStruct(mix.shape, F32),
            jax.ShapeDtypeStruct((channels // LANES, MSG_ROWS, LANES), BF16),
        ],
        scratch_shapes=[
            pltpu.VMEM((2, 8 + block, tile), F32),
            pltpu.VMEM((2, NST, NST * block), BF16),
        ],
        compiler_params=pltpu.CompilerParams(vmem_limit_bytes=VMEM),
        cost_estimate=pl.CostEstimate(flops=10**8, bytes_accessed=7 * 10**6, transcendentals=9 * 10**6),
        name="summarize",
    )(info, before, after, tail, mix, step, bias, taps, conv_bias, decay_log, writes)


def prefix_kernel(info_ref, msg_ref, decay_ref, out_ref, *, pairs):
    del info_ref
    decay = -jnp.exp(decay_ref[...]) * LOG2E

    def hop(j, state, half):
        out_ref[j, half * NST:(half + 1) * NST] = state.astype(BF16)
        piece = msg_ref[j].astype(F32)
        end = piece[2 * NST + 2 * half:2 * NST + 2 * half + 1] + piece[2 * NST + 2 * half + 1:2 * NST + 2 * half + 2]
        return jnp.exp2(decay * end) * state + piece[half * NST:(half + 1) * NST]

    state = jnp.zeros(decay.shape, F32)
    state = lax.fori_loop(0, pairs, lambda j, s: hop(j, s, 0), state, unroll=8)
    lax.fori_loop(0, pairs, lambda j, s: hop(pairs - 1 - j, s, 1), state, unroll=8)


def prefix(info, msg, decay_log):
    pairs = msg.shape[0]
    return pl.pallas_call(
        functools.partial(prefix_kernel, pairs=pairs),
        grid_spec=pltpu.PrefetchScalarGridSpec(
            num_scalar_prefetch=1,
            grid=(1,),
            in_specs=[
                pl.BlockSpec(msg.shape, lambda i, info: (0, 0, 0)),
                pl.BlockSpec((NST, LANES), lambda i, info: (0, info[5])),
            ],
            out_specs=pl.BlockSpec((pairs, 2 * NST, LANES), lambda i, info: (0, 0, 0)),
        ),
        out_shape=jax.ShapeDtypeStruct((pairs, 2 * NST, LANES), BF16),
        cost_estimate=pl.CostEstimate(flops=10**6, bytes_accessed=6 * 10**5, transcendentals=10**5),
        compiler_params=pltpu.CompilerParams(vmem_limit_bytes=SMALL),
        name="prefix",
    )(info, msg, decay_log)


def scan_kernel(
    rate_ref, signal_ref, gate_ref, start_ref, decay_ref, skip_ref, writes_ref, reads_ref,
    out_ref, inflow, held, mats, wide, *, block
):
    tile = rate_ref.shape[2]
    cols = tile // LANES
    group = 16
    decay = -jnp.exp(decay_ref[...]) * LOG2E

    @pl.when(pl.program_id(0) == 0)
    def _():
        for b in range(2):
            across = writes_ref[b].astype(F32)
            turned = jnp.transpose(reads_ref[b].astype(F32))
            for t in range(block):
                wide[b, t] = jnp.broadcast_to(across[:, t:t + 1], (NST, LANES))
            for g in range(block // group):
                rows = turned[g * group:(g + 1) * group]
                spread = jnp.concatenate([rows] * group, axis=1)
                token = lax.broadcasted_iota(jnp.int32, spread.shape, 0)
                owner = lax.broadcasted_iota(jnp.int32, spread.shape, 1) // NST
                mats[b, g] = jnp.where(token == owner, spread, 0.0).astype(BF16)

    for b in range(2):
        inflow[b] = rate_ref[b] * signal_ref[b]

    def start(b):
        return jnp.concatenate(
            [start_ref[j, b * NST:(b + 1) * NST].astype(F32) for j in range(cols)], axis=1
        )

    def some(g, states):
        states = list(states)
        for k in range(group):
            t = g * group + k
            for b in range(2):
                kept = jnp.exp2(decay * rate_ref[b, pl.ds(t, 1)])
                write = jnp.concatenate([wide[b, t]] * cols, axis=1)
                states[b] = kept * states[b] + inflow[b, pl.ds(t, 1)] * write
                held[b, t * NST:(t + 1) * NST] = states[b].astype(BF16)
        at = g * group
        for b in range(2):
            summed = dot_nn(mats[b, g], held[b, at * NST:(at + group) * NST])
            mixed = summed + skip_ref[...] * signal_ref[b, pl.ds(at, group)]
            gate = gate_ref[b, pl.ds(at, group)].astype(F32)
            out_ref[b, pl.ds(at, group)] = (mixed * silu(gate)).astype(BF16)
        return tuple(states)

    states = (start(0), start(1))
    for g in range(block // group):
        states = some(g, states)


def scan(rate, signal, gate, start, decay_log, skip, writes, reads):
    _, block, channels = rate.shape
    tile = min(TILE, channels)
    seq = pl.BlockSpec((2, block, tile), lambda c: (0, 0, c))
    line = lambda rows: pl.BlockSpec((rows, tile), lambda c: (0, c))
    return pl.pallas_call(
        functools.partial(scan_kernel, block=block),
        grid=(channels // tile,),
        in_specs=[
            seq,
            seq,
            seq,
            pl.BlockSpec((tile // LANES, 2 * NST, LANES), lambda c: (c, 0, 0)),
            line(NST),
            line(1),
            pl.BlockSpec(writes.shape, lambda c: (0, 0, 0)),
            pl.BlockSpec(reads.shape, lambda c: (0, 0, 0)),
        ],
        out_specs=seq,
        out_shape=jax.ShapeDtypeStruct(gate.shape, BF16),
        scratch_shapes=[
            pltpu.VMEM((2, block, tile), F32),
            pltpu.VMEM((2, block * NST, tile), BF16),
            pltpu.VMEM((2, block // 16, 16, 16 * NST), BF16),
            pltpu.VMEM((2, block, NST, LANES), F32),
        ],
        compiler_params=pltpu.CompilerParams(vmem_limit_bytes=VMEM),
        cost_estimate=pl.CostEstimate(flops=10**8, bytes_accessed=8 * 10**6, transcendentals=9 * 10**6),
        name="scan",
    )(rate, signal, gate, start, decay_log, skip, writes, reads)


def body(
    queries,
    projected_key_rows,
    values,
    mixer_input,
    step_raw,
    gate_input,
    state_write,
    state_read,
    decay_log,
    step_bias,
    conv_weight,
    conv_bias,
    skip_gain,
):
    rank = lax.axis_index("ctx")
    count = lax.axis_size("ctx")
    block = queries.shape[2]
    taps = conv_weight.shape[0]

    halves = mixer_input[0]
    tails = halves[:, block - (taps - 1):]
    forward = [(i, i + 1) for i in range(count - 1)]
    backward = [(i + 1, i) for i in range(count - 1)]
    before_first = lax.ppermute(tails[0], "ctx", forward)
    before_second = lax.ppermute(tails[1], "ctx", backward)

    row, place = rank // ROW, rank % ROW
    core, odd = lax.axis_index("dp") % 2, row % 2
    info = jnp.stack(
        [2 * core + odd, 2 * core + 1 - odd, place, odd, core, rank, (rank == count - 1).astype(rank.dtype)]
    ).astype(jnp.int32)
    swaps = [[], []]
    for k in range(2):
        for dp in range(lax.axis_size("dp")):
            for ctx in range(count):
                x, z = ctx // ROW, ctx % ROW
                target = (dp // 2 * 2 + x // 2) * count + (dp % 2 * 2 + (x % 2 ^ k)) * ROW + z
                swaps[k].append((dp * count + ctx, target))
    gathers = [
        [(pair * 2 + c) * count + x * ROW + z for c in range(2) for z in range(ROW)]
        for pair in range(lax.axis_size("dp") // 2)
        for x in range(count // ROW)
    ]

    def swap(array):
        width = array.shape[-1] // 2
        low, high = array[..., :width], array[..., width:]
        parts = [jnp.where(odd == k, low, high) for k in range(2)]
        return [lax.ppermute(part, ("dp", "ctx"), pairs) for part, pairs in zip(parts, swaps)]

    def swap_back(k, array):
        return lax.ppermute(array, ("dp", "ctx"), [(t, f) for f, t in swaps[k]])

    parts = split(info, projected_key_rows[0], values[0])
    parts = [lax.ppermute(part, ("dp", "ctx"), pairs) for part, pairs in zip(parts, swaps)]
    kv = pack(*parts, before_first, before_second)
    kv = lax.all_gather(kv, ("dp", "ctx"), axis_index_groups=gathers)
    asked = swap(queries[0])

    write = jnp.swapaxes(state_write[0], 1, 2)
    read = jnp.swapaxes(state_read[0], 1, 2)
    rate, signal, msg = summarize(
        info, before_first, before_second, tails[0], halves, step_raw[0], step_bias[None], conv_weight,
        conv_bias[None], decay_log, write,
    )
    msg = lax.all_to_all(msg, "ctx", 0, 0, tiled=True)
    start = prefix(info, msg, decay_log)
    start = lax.all_to_all(start, "ctx", 0, 0, tiled=True)
    selected = scan(rate, signal, gate_input[0], start, decay_log, skip_gain[None], write, read)
    answers = []
    for k in range(2):
        answers.append(swap_back(k, attend(info, k, asked[k], kv)))
    low = jnp.where(odd == 0, answers[0], answers[1])
    high = jnp.where(odd == 0, answers[1], answers[0])
    attended = jnp.concatenate([low, high], axis=-1)
    return (attended[None], selected[None])


def solution(mesh):
    rows = P(("dp", "ctx"), None, None, "tp")
    shared = P(("dp", "ctx"), None, None, None)
    return jax.shard_map(
        body,
        mesh=mesh,
        in_specs=(rows,) * 6 + (shared,) * 2
        + (P(None, "tp"), P("tp"), P(None, "tp"), P("tp"), P("tp")),
        out_specs=(rows, rows),
        check_vma=False,
    )
```

```python
import functools

import jax
import jax.numpy as jnp
from jax import lax
from jax.experimental import pallas as pl
from jax.experimental.pallas import tpu as pltpu
from jax.sharding import PartitionSpec as P

HEAD = 128
NST = 16
LOG2E = 1.4426950408889634
TILE = 512
WIDE = 1024
LANES = 128
MSG_ROWS = 40
ROW = 8
BIG_NEG = -1e30
VMEM = 56 * 2**20
SMALL = 8 * 2**20
F32 = jnp.float32
BF16 = jnp.bfloat16


def dot_nt(a, b):
    return lax.dot_general(a, b, (((1,), (1,)), ((), ())), preferred_element_type=F32)


def dot_nn(a, b):
    return lax.dot_general(a, b, (((1,), (0,)), ((), ())), preferred_element_type=F32)


def attend_kernel(where_ref, q_ref, kv_ref, o_ref, qs, acc, top, kvs, sems, *, block, heads, turns, turn):
    mine, place, odd = where_ref[turn], where_ref[2], where_ref[3]
    rows = heads * block
    span = ROW * block
    scale = LOG2E * HEAD ** -0.5

    def fetch(row):
        source = kv_ref.at[pl.ds((row // 2) * ROW, ROW), (row + odd) % 2]
        return pltpu.make_async_copy(source, kvs.at[row], sems.at[row])

    for d in range(turns):
        fetch((mine + d) % turns).start()

    for b in range(2):
        for h in range(heads):
            scaled = q_ref[b, :, h * HEAD:(h + 1) * HEAD].astype(F32) * scale
            high = scaled.astype(BF16)
            low = (scaled - high.astype(F32)).astype(BF16)
            qs[pl.ds(b * rows + h * block, block), :HEAD] = high
            qs[pl.ds(b * rows + h * block, block), HEAD:] = low

    def score(b, row, half):
        keys = kvs[row, :, 0, half].reshape(span, HEAD)
        at = pl.multiple_of(b * rows, rows)
        return dot_nt(qs[pl.ds(at, rows)], jnp.concatenate([keys, keys], axis=1))

    def update(b, row, half, scores, first):
        vals = kvs[row, :, 1, half].reshape(span, HEAD)
        at = pl.multiple_of(b * rows, rows)
        best = jnp.broadcast_to(jnp.max(scores, axis=1, keepdims=True), (rows, LANES))
        if not first:
            old = top[pl.ds(at, rows)]
            best = jnp.maximum(best, old)
        weights = jnp.exp2(scores - jnp.concatenate([best] * (span // LANES), axis=1)).astype(BF16)
        added = dot_nn(weights, jnp.concatenate([vals, jnp.ones_like(vals)], axis=1))
        if not first:
            factor = jnp.exp2(old - best)
            added = added + acc[pl.ds(at, rows)] * jnp.concatenate([factor, factor], axis=1)
        acc[pl.ds(at, rows)] = added
        top[pl.ds(at, rows)] = best

    token = lax.broadcasted_iota(jnp.int32, (rows, span), 0) % block
    key = lax.broadcasted_iota(jnp.int32, (rows, span), 1)
    upto = key <= token + place * block
    after = (key >= (place + 1) * block) | ((key >= place * block) & upto)

    fetch(mine).wait()
    early = score(0, mine, 0)
    late = score(1, mine, 0)
    own = score(1, mine, 1)
    update(0, mine, 0, jnp.where(upto, early, BIG_NEG), True)
    update(1, mine, 0, late, True)
    update(1, mine, 1, jnp.where(after, own, BIG_NEG), False)

    def other(d, carry):
        row = (mine + d) % turns
        later = (row > mine).astype(jnp.int32)
        fetch(row).wait()
        late = score(1, row, 0)
        second = score(later, row, later)
        update(1, row, 0, late, False)
        update(later, row, later, second, False)
        return carry

    lax.fori_loop(1, turns, other, 0)
    for b in range(2):
        for h in range(heads):
            done = acc[pl.ds(b * rows + h * block, block)]
            o_ref[b, :, h * HEAD:(h + 1) * HEAD] = (done[:, :HEAD] / done[:, HEAD:]).astype(BF16)


def attend(where, turn, queries, kv):
    _, block, width = queries.shape
    heads = width // HEAD
    turns = 2 * kv.shape[0] // ROW
    return pl.pallas_call(
        functools.partial(attend_kernel, block=block, heads=heads, turns=turns, turn=turn),
        in_specs=[
            pl.BlockSpec(memory_space=pltpu.SMEM),
            pl.BlockSpec(memory_space=pltpu.VMEM),
            pl.BlockSpec(memory_space=pl.ANY),
        ],
        out_specs=pl.BlockSpec(memory_space=pltpu.VMEM),
        scratch_shapes=[
            pltpu.VMEM((2 * heads * block, 2 * HEAD), BF16),
            pltpu.VMEM((2 * heads * block, 2 * HEAD), F32),
            pltpu.VMEM((2 * heads * block, LANES), F32),
            pltpu.VMEM((turns, ROW, 2, 2, block, HEAD), BF16),
            pltpu.SemaphoreType.DMA((turns,)),
        ],
        out_shape=jax.ShapeDtypeStruct(queries.shape, BF16),
        compiler_params=pltpu.CompilerParams(vmem_limit_bytes=24 * 2**20),
        cost_estimate=pl.CostEstimate(flops=10**9, bytes_accessed=3 * 10**6, transcendentals=3 * 10**6),
        name="attend",
    )(where, queries, kv)


def split_kernel(odd_ref, keys_ref, values_ref, first_ref, second_ref):
    odd = odd_ref[3]
    for k, out in enumerate((first_ref, second_ref)):
        at = pl.multiple_of(((odd + k) % 2) * HEAD, HEAD)
        out[0] = keys_ref[:, :, pl.ds(at, HEAD)]
        out[1] = values_ref[:, :, pl.ds(at, HEAD)]


def split(odd, keys, values):
    half, block, _ = keys.shape
    part = jax.ShapeDtypeStruct((2, half, block, HEAD), BF16)
    return pl.pallas_call(
        split_kernel,
        in_specs=[pl.BlockSpec(memory_space=pltpu.SMEM)] + [pl.BlockSpec(memory_space=pltpu.VMEM)] * 2,
        out_specs=[pl.BlockSpec(memory_space=pltpu.VMEM)] * 2,
        out_shape=[part, part],
        compiler_params=pltpu.CompilerParams(vmem_limit_bytes=VMEM),
        name="split",
    )(odd, keys, values)


def pack_kernel(first_ref, second_ref, before_ref, after_ref, pair_ref):
    del before_ref, after_ref
    pair_ref[0] = first_ref[...]
    pair_ref[1] = second_ref[...]


def pack(first, second, before, after):
    vmem = pl.BlockSpec(memory_space=pltpu.VMEM)
    anywhere = pl.BlockSpec(memory_space=pl.ANY)
    return pl.pallas_call(
        pack_kernel,
        in_specs=[vmem] * 2 + [anywhere] * 2,
        out_specs=vmem,
        out_shape=jax.ShapeDtypeStruct((2,) + first.shape, BF16),
        compiler_params=pltpu.CompilerParams(vmem_limit_bytes=SMALL),
        name="pack",
    )(first, second, before, after)


def softplus(v):
    small = jnp.exp(-jnp.abs(v))
    return jnp.maximum(v, 0.0) + jnp.log1p(small)


def silu(v):
    half = 0.5 * v
    return half + half * jnp.tanh(half)


def summary_kernel(
    info_ref, before_ref, after_ref, tail_ref, mix_ref, step_ref, bias_ref, taps_ref, conv_bias_ref, decay_ref, writes_ref,
    rate_ref, signal_ref, msg_ref, ext, spread, *, block, taps
):
    decay = -jnp.exp(decay_ref[...]) * LOG2E

    @pl.when(pl.program_id(0) == 0)
    def _():
        for b in range(2):
            across = writes_ref[b].astype(F32)
            wide = jnp.concatenate([across] * NST, axis=1)
            state = lax.broadcasted_iota(jnp.int32, wide.shape, 0)
            owner = lax.broadcasted_iota(jnp.int32, wide.shape, 1) // block
            spread[b] = jnp.where(state == owner, wide, 0.0).astype(BF16)

    row = lax.broadcasted_iota(jnp.int32, (block, 2 * block), 0)
    col = lax.broadcasted_iota(jnp.int32, (block, 2 * block), 1) % block
    later = (col > row).astype(BF16)
    follow = jnp.where(info_ref[6] == 1, tail_ref[...].astype(F32), after_ref[...].astype(F32))
    halos = (before_ref[...].astype(F32), follow)
    states, ends = [], []
    for b in range(2):
        ext[b, 8 - taps + 1:8] = halos[b]
        ext[b, 8:] = mix_ref[b].astype(F32)
        summed = conv_bias_ref[...]
        for m in range(taps):
            summed = summed + taps_ref[m:m + 1] * ext[b, pl.ds(8 - taps + 1 + m, block)]
        signal = silu(summed)
        rate = softplus(step_ref[b].astype(F32) + bias_ref[...])
        rate_ref[b] = rate
        signal_ref[b] = signal
        inflow = (rate * signal).astype(BF16)
        high = rate.astype(BF16)
        low = (rate - high.astype(F32)).astype(BF16)
        remaining = dot_nn(later, jnp.concatenate([high, low], axis=0))
        ends.append(remaining[:1] + rate[:1])
        state = 0.0
        for g in range(0, NST, 4):
            kept = [
                jnp.exp2(decay[n:n + 1] * remaining).astype(BF16) * inflow for n in range(g, g + 4)
            ]
            part = spread[b, :, g * block:(g + 4) * block]
            state = state + dot_nn(part, jnp.concatenate(kept, axis=0))
        states.append(state)
    rows = []
    for end in ends:
        high = end.astype(BF16).astype(F32)
        rows += [high, end - high]
    rows.append(jnp.zeros((8 - len(rows), rows[0].shape[1]), F32))
    message = jnp.concatenate(states + rows, axis=0).astype(BF16)
    for j in range(message.shape[1] // LANES):
        msg_ref[j] = message[:, j * LANES:(j + 1) * LANES]


def summarize(info, before, after, tail, mix, step, bias, taps, conv_bias, decay_log, writes):
    _, block, channels = mix.shape
    tile = min(WIDE, channels)
    seq = pl.BlockSpec((2, block, tile), lambda c: (0, 0, c))
    line = lambda rows: pl.BlockSpec((rows, tile), lambda c: (0, c))
    return pl.pallas_call(
        functools.partial(summary_kernel, block=block, taps=taps.shape[0]),
        grid=(channels // tile,),
        in_specs=[
            pl.BlockSpec(memory_space=pltpu.SMEM),
            line(before.shape[0]),
            line(before.shape[0]),
            line(before.shape[0]),
            seq,
            seq,
            line(1),
            line(taps.shape[0]),
            line(1),
            line(NST),
            pl.BlockSpec(writes.shape, lambda c: (0, 0, 0)),
        ],
        out_specs=[seq, seq, pl.BlockSpec((tile // LANES, MSG_ROWS, LANES), lambda c: (c, 0, 0))],
        out_shape=[
            jax.ShapeDtypeStruct(mix.shape, F32),
            jax.ShapeDtypeStruct(mix.shape, F32),
            jax.ShapeDtypeStruct((channels // LANES, MSG_ROWS, LANES), BF16),
        ],
        scratch_shapes=[
            pltpu.VMEM((2, 8 + block, tile), F32),
            pltpu.VMEM((2, NST, NST * block), BF16),
        ],
        compiler_params=pltpu.CompilerParams(vmem_limit_bytes=VMEM),
        cost_estimate=pl.CostEstimate(flops=10**8, bytes_accessed=7 * 10**6, transcendentals=9 * 10**6),
        name="summarize",
    )(info, before, after, tail, mix, step, bias, taps, conv_bias, decay_log, writes)


def prefix_kernel(info_ref, msg_ref, decay_ref, out_ref, *, pairs):
    del info_ref
    decay = -jnp.exp(decay_ref[...]) * LOG2E

    def hop(j, state, half):
        out_ref[j, half * NST:(half + 1) * NST] = state.astype(BF16)
        piece = msg_ref[j].astype(F32)
        end = piece[2 * NST + 2 * half:2 * NST + 2 * half + 1] + piece[2 * NST + 2 * half + 1:2 * NST + 2 * half + 2]
        return jnp.exp2(decay * end) * state + piece[half * NST:(half + 1) * NST]

    state = jnp.zeros(decay.shape, F32)
    state = lax.fori_loop(0, pairs, lambda j, s: hop(j, s, 0), state, unroll=8)
    lax.fori_loop(0, pairs, lambda j, s: hop(pairs - 1 - j, s, 1), state, unroll=8)


def prefix(info, msg, decay_log):
    pairs = msg.shape[0]
    return pl.pallas_call(
        functools.partial(prefix_kernel, pairs=pairs),
        grid_spec=pltpu.PrefetchScalarGridSpec(
            num_scalar_prefetch=1,
            grid=(1,),
            in_specs=[
                pl.BlockSpec(msg.shape, lambda i, info: (0, 0, 0)),
                pl.BlockSpec((NST, LANES), lambda i, info: (0, info[5])),
            ],
            out_specs=pl.BlockSpec((pairs, 2 * NST, LANES), lambda i, info: (0, 0, 0)),
        ),
        out_shape=jax.ShapeDtypeStruct((pairs, 2 * NST, LANES), BF16),
        cost_estimate=pl.CostEstimate(flops=10**6, bytes_accessed=6 * 10**5, transcendentals=10**5),
        compiler_params=pltpu.CompilerParams(vmem_limit_bytes=SMALL),
        name="prefix",
    )(info, msg, decay_log)


def scan_kernel(
    rate_ref, signal_ref, gate_ref, start_ref, decay_ref, skip_ref, writes_ref, reads_ref,
    out_ref, inflow, held, mats, wide, *, block
):
    tile = rate_ref.shape[2]
    cols = tile // LANES
    group = 16
    decay = -jnp.exp(decay_ref[...]) * LOG2E

    @pl.when(pl.program_id(0) == 0)
    def _():
        for b in range(2):
            across = writes_ref[b].astype(F32)
            turned = jnp.transpose(reads_ref[b].astype(F32))
            for t in range(block):
                wide[b, t] = jnp.broadcast_to(across[:, t:t + 1], (NST, LANES))
            for g in range(block // group):
                rows = turned[g * group:(g + 1) * group]
                spread = jnp.concatenate([rows] * group, axis=1)
                token = lax.broadcasted_iota(jnp.int32, spread.shape, 0)
                owner = lax.broadcasted_iota(jnp.int32, spread.shape, 1) // NST
                mats[b, g] = jnp.where(token == owner, spread, 0.0).astype(BF16)

    for b in range(2):
        inflow[b] = rate_ref[b] * signal_ref[b]

    def start(b):
        return jnp.concatenate(
            [start_ref[j, b * NST:(b + 1) * NST].astype(F32) for j in range(cols)], axis=1
        )

    def some(g, states):
        states = list(states)
        for k in range(group):
            t = g * group + k
            for b in range(2):
                kept = jnp.exp2(decay * rate_ref[b, pl.ds(t, 1)])
                write = jnp.concatenate([wide[b, t]] * cols, axis=1)
                states[b] = kept * states[b] + inflow[b, pl.ds(t, 1)] * write
                held[b, t * NST:(t + 1) * NST] = states[b].astype(BF16)
        at = g * group
        for b in range(2):
            summed = dot_nn(mats[b, g], held[b, at * NST:(at + group) * NST])
            mixed = summed + skip_ref[...] * signal_ref[b, pl.ds(at, group)]
            gate = gate_ref[b, pl.ds(at, group)].astype(F32)
            out_ref[b, pl.ds(at, group)] = (mixed * silu(gate)).astype(BF16)
        return tuple(states)

    states = (start(0), start(1))
    for g in range(block // group):
        states = some(g, states)


def scan(rate, signal, gate, start, decay_log, skip, writes, reads):
    _, block, channels = rate.shape
    tile = min(TILE, channels)
    seq = pl.BlockSpec((2, block, tile), lambda c: (0, 0, c))
    line = lambda rows: pl.BlockSpec((rows, tile), lambda c: (0, c))
    return pl.pallas_call(
        functools.partial(scan_kernel, block=block),
        grid=(channels // tile,),
        in_specs=[
            seq,
            seq,
            seq,
            pl.BlockSpec((tile // LANES, 2 * NST, LANES), lambda c: (c, 0, 0)),
            line(NST),
            line(1),
            pl.BlockSpec(writes.shape, lambda c: (0, 0, 0)),
            pl.BlockSpec(reads.shape, lambda c: (0, 0, 0)),
        ],
        out_specs=seq,
        out_shape=jax.ShapeDtypeStruct(gate.shape, BF16),
        scratch_shapes=[
            pltpu.VMEM((2, block, tile), F32),
            pltpu.VMEM((2, block * NST, tile), BF16),
            pltpu.VMEM((2, block // 16, 16, 16 * NST), BF16),
            pltpu.VMEM((2, block, NST, LANES), F32),
        ],
        compiler_params=pltpu.CompilerParams(vmem_limit_bytes=VMEM),
        cost_estimate=pl.CostEstimate(flops=10**8, bytes_accessed=8 * 10**6, transcendentals=9 * 10**6),
        name="scan",
    )(rate, signal, gate, start, decay_log, skip, writes, reads)


def body(
    queries,
    projected_key_rows,
    values,
    mixer_input,
    step_raw,
    gate_input,
    state_write,
    state_read,
    decay_log,
    step_bias,
    conv_weight,
    conv_bias,
    skip_gain,
):
    rank = lax.axis_index("ctx")
    count = lax.axis_size("ctx")
    block = queries.shape[2]
    taps = conv_weight.shape[0]

    halves = mixer_input[0]
    tails = halves[:, block - (taps - 1):]
    forward = [(i, i + 1) for i in range(count - 1)]
    backward = [(i + 1, i) for i in range(count - 1)]
    before_first = lax.ppermute(tails[0], "ctx", forward)
    before_second = lax.ppermute(tails[1], "ctx", backward)

    row, place = rank // ROW, rank % ROW
    core, odd = lax.axis_index("dp") % 2, row % 2
    info = jnp.stack(
        [2 * core + odd, 2 * core + 1 - odd, place, odd, core, rank, (rank == count - 1).astype(rank.dtype)]
    ).astype(jnp.int32)
    swaps = [[], []]
    for k in range(2):
        for dp in range(lax.axis_size("dp")):
            for ctx in range(count):
                x, z = ctx // ROW, ctx % ROW
                target = (dp // 2 * 2 + x // 2) * count + (dp % 2 * 2 + (x % 2 ^ k)) * ROW + z
                swaps[k].append((dp * count + ctx, target))
    gathers = [
        [(pair * 2 + c) * count + x * ROW + z for c in range(2) for z in range(ROW)]
        for pair in range(lax.axis_size("dp") // 2)
        for x in range(count // ROW)
    ]

    def swap(array):
        width = array.shape[-1] // 2
        low, high = array[..., :width], array[..., width:]
        parts = [jnp.where(odd == k, low, high) for k in range(2)]
        return [lax.ppermute(part, ("dp", "ctx"), pairs) for part, pairs in zip(parts, swaps)]

    def swap_back(k, array):
        return lax.ppermute(array, ("dp", "ctx"), [(t, f) for f, t in swaps[k]])

    parts = split(info, projected_key_rows[0], values[0])
    parts = [lax.ppermute(part, ("dp", "ctx"), pairs) for part, pairs in zip(parts, swaps)]
    kv = pack(*parts, before_first, before_second)
    kv = lax.all_gather(kv, ("dp", "ctx"), axis_index_groups=gathers)
    asked = swap(queries[0])

    write = jnp.swapaxes(state_write[0], 1, 2)
    read = jnp.swapaxes(state_read[0], 1, 2)
    rate, signal, msg = summarize(
        info, before_first, before_second, tails[0], halves, step_raw[0], step_bias[None], conv_weight,
        conv_bias[None], decay_log, write,
    )
    msg = lax.all_to_all(msg, "ctx", 0, 0, tiled=True)
    start = prefix(info, msg, decay_log)
    start = lax.all_to_all(start, "ctx", 0, 0, tiled=True)
    selected = scan(rate, signal, gate_input[0], start, decay_log, skip_gain[None], write, read)
    answers = []
    for k in range(2):
        answers.append(swap_back(k, attend(info, k, asked[k], kv)))
    low = jnp.where(odd == 0, answers[0], answers[1])
    high = jnp.where(odd == 0, answers[1], answers[0])
    attended = jnp.concatenate([low, high], axis=-1)
    return (attended[None], selected[None])


def solution(mesh):
    rows = P(("dp", "ctx"), None, None, "tp")
    shared = P(("dp", "ctx"), None, None, None)
    return jax.shard_map(
        body,
        mesh=mesh,
        in_specs=(rows,) * 6 + (shared,) * 2
        + (P(None, "tp"), P("tp"), P(None, "tp"), P("tp"), P("tp")),
        out_specs=(rows, rows),
        check_vma=False,
    )
```
